512 devices in a mesh: seq: 64 (over y_lo, z, x), uly: 8 (over y_hi, core).
Axes of the slice: x: 4, y: 8 (y_hi: 4, y_lo: 2; y = y_hi * 2 + y_lo), z: 8, core: 2. Of those that a mesh axis runs over, the one named last changes fastest.
Arguments:
- queries: bfloat16 [2, 32768, 2048], P(None, ('seq', 'uly')), may hold values from -22.5 to 22.5
- keys: bfloat16 [2, 32768, 2048], P(None, ('seq', 'uly')), may hold values from -22.5 to 22.5
- values: bfloat16 [2, 32768, 2048], P(None, ('seq', 'uly')), may hold values from -6 to 6
- query_tan: bfloat16 [2, 32768, 2048], P(None, ('seq', 'uly')), may hold values from -6 to 6
- key_tan: bfloat16 [2, 32768, 2048], P(None, ('seq', 'uly')), may hold values from -6 to 6
- value_tan: bfloat16 [2, 32768, 2048], P(None, ('seq', 'uly')), may hold values from -6 to 6
- weight_out: float32 [2048, 1536], P(None, 'seq'), may hold values from -0.125 to 0.125
- gate: float32 [2, 1536], replicated, may hold values from -5 to 5
- gate_tan: float32 [2, 1536], replicated, may hold values from -5 to 5
- cotangent: bfloat16 [2, 32768, 1536], P(None, ('seq', 'uly')), may hold values from -24 to 24
Outputs:
- mixed: bfloat16 [2, 32768, 1536], P(None, ('seq', 'uly'))
- mixed_tan: bfloat16 [2, 32768, 1536], P(None, ('seq', 'uly'))
- weight_grad: float32 [2048, 1536], P('uly', 'seq')
The draws below stay inside these ranges and needn't reach their ends.
All inputs are finite; a program needn't handle non-finite values.
Results may differ from the reference program's by a relative error of at most 0.0064.
Values may be sent and summed in bfloat16 or wider, within the bound.
No kernel may reach another device: no remote copies, remote signals or barrier semaphores. Data moves between devices by JAX's collectives and lax.ppermute only.
A program may use at most 64 MiB of HBM per device.

```python
import jax
import jax.numpy as jnp
from jax import lax

D = 1536
HD = 128
SEQS = 2
F = 2048
RADIUS = 128
LEN = 32768


def drawn_rows(key):
    return jnp.clip(jax.random.normal(key, (SEQS, LEN, F), jnp.float32), -4.5, 4.5)


def draw_queries(key, part):
    key = jax.random.fold_in(key, 3)
    result = drawn_rows(key)
    return result.astype(jnp.bfloat16)


def draw_keys(key, part):
    key = jax.random.fold_in(key, 7)
    result = drawn_rows(key)
    return result.astype(jnp.bfloat16)


def spiked(values, stream_key, source, target, parts, factor):
    def block_of(position):
        return (jnp.arange(values.shape[position]) // (values.shape[position] // parts)).reshape((-1,) + (1,) * (values.ndim - 1 - position))

    near = jax.random.permutation(stream_key, parts)[block_of(target)]
    other_side = (block_of(target) + parts // 2) % parts
    return jnp.where((block_of(source) == near) | (block_of(source) == other_side), factor * values, values)


def block_scale(stream_key, dims, shards, smallest, top_value):
    factor_of = 1.0
    for dim, blocks in shards:
        heights = jax.random.uniform(jax.random.fold_in(jax.random.fold_in(stream_key, 6), dim), (blocks,), jnp.float32, smallest / len(shards), top_value / len(shards))
        factor_of = factor_of * jnp.repeat(jnp.exp(heights), dims[dim] // blocks).reshape((-1,) + (1,) * (len(dims) - 1 - dim))
    return factor_of


def bell_draw(stream_key, shape, width, most, cuts=(), held_as=jnp.bfloat16):
    entries = width * jax.random.normal(stream_key, shape, jnp.float32)
    if cuts:
        entries = entries * block_scale(stream_key, shape, cuts, -0.22, 0.18)
    return jnp.clip(entries, -most, most).astype(held_as)


def bell_draw_with(stream_key, dims, width, bound, cuts, heavy, kind=jnp.bfloat16):
    values = width * jax.random.normal(stream_key, dims, jnp.float32)
    if cuts:
        values = values * block_scale(stream_key, dims, cuts, -0.22, 0.18)
    return jnp.clip(spiked(values, jax.random.fold_in(stream_key, 3), *heavy), -bound, bound).astype(kind)


def setup_inputs(seed: int = 0) -> dict:
    key_list = jax.random.split(jax.random.key(seed), 11)
    return {
        "queries": draw_queries(jax.random.fold_in(key_list[10], 71), 0),
        "keys": draw_keys(jax.random.fold_in(key_list[10], 71), 0),
        "values": bell_draw(key_list[2], (SEQS, LEN, F), 1.0, 6.0, ((1, 512),)),
        "query_tan": bell_draw(key_list[3], (SEQS, LEN, F), 1.0, 6.0, ((1, 512),)),
        "key_tan": bell_draw(key_list[4], (SEQS, LEN, F), 1.0, 6.0, ((1, 512),)),
        "value_tan": bell_draw(key_list[5], (SEQS, LEN, F), 1.0, 6.0, ((1, 512),)),
        "weight_out": bell_draw(key_list[6], (F, D), F ** -0.5, 0.125, ((1, 64),), jnp.float32),
        "gate": bell_draw(key_list[7], (SEQS, D), 1.0, 5.0, (), jnp.float32),
        "gate_tan": bell_draw(key_list[8], (SEQS, D), 1.0, 5.0, (), jnp.float32),
        "cotangent": bell_draw_with(key_list[9], (SEQS, LEN, D), 1.0, 24.0, ((1, 512),), (1, 2, 512, 6.0)),
    }


def contract(form, left, right):
    return jnp.einsum(form, left, right, precision=lax.Precision.HIGHEST, preferred_element_type=jnp.float32)


def attend_block(query_blk, key_blk, value_blk, query_tan_blk, key_tan_blk, value_tan_blk, allowed):
    score_scale = HD ** -0.5
    scores = contract("sqhd,skhd->shqk", query_blk, key_blk) * score_scale
    scores = jnp.where(allowed, scores, -1e30)
    row_top = jnp.max(scores, axis=-1, keepdims=True)
    exp_terms = jnp.where(allowed, jnp.exp(scores - row_top), 0.0)
    probs_full = exp_terms / jnp.sum(exp_terms, axis=-1, keepdims=True)
    score_tan = (contract("sqhd,skhd->shqk", query_tan_blk, key_blk) + contract("sqhd,skhd->shqk", query_blk, key_tan_blk)) * score_scale
    probs_tan = probs_full * (score_tan - jnp.sum(probs_full * score_tan, axis=-1, keepdims=True))
    probs_low = lax.optimization_barrier(probs_full.astype(jnp.bfloat16)).astype(jnp.float32)
    probs_tan_low = lax.optimization_barrier(probs_tan.astype(jnp.bfloat16)).astype(jnp.float32)
    attended = contract("shqk,skhd->sqhd", probs_low, value_blk)
    attended_tan = contract("shqk,skhd->sqhd", probs_tan_low, value_blk) + contract("shqk,skhd->sqhd", probs_low, value_tan_blk)
    return attended.astype(jnp.bfloat16), attended_tan.astype(jnp.bfloat16)


def windowed_attention(queries, keys, values, query_tan, key_tan, value_tan):
    seq_count, length, full_width = queries.shape
    head_count = full_width // HD
    block_len = 2 * RADIUS
    key_span = block_len + 2 * RADIUS

    def by_head(tensor):
        return tensor.reshape(seq_count, tensor.shape[1], head_count, HD)

    def padded(tensor):
        return jnp.pad(by_head(tensor), ((0, 0), (RADIUS, RADIUS), (0, 0), (0, 0)))

    query_heads = by_head(queries)
    query_tan_heads = by_head(query_tan)
    key_pad = padded(keys)
    value_pad = padded(values)
    key_tan_pad = padded(key_tan)
    value_tan_pad = padded(value_tan)
    row_ids = jnp.arange(block_len, dtype=jnp.int32)
    key_ids = jnp.arange(key_span, dtype=jnp.int32)
    nearby = jnp.abs(row_ids[:, None] + RADIUS - key_ids[None, :]) <= RADIUS

    def one_block(block_idx):
        first_pos = (block_idx * block_len).astype(jnp.int32)
        key_pos = first_pos - RADIUS + key_ids
        allowed = nearby & ((key_pos >= 0) & (key_pos < length))[None, :]

        def rows_of(tensor, row_count):
            return lax.dynamic_slice_in_dim(tensor, first_pos, row_count, 1).astype(jnp.float32)

        return attend_block(rows_of(query_heads, block_len), rows_of(key_pad, key_span), rows_of(value_pad, key_span),
                            rows_of(query_tan_heads, block_len), rows_of(key_tan_pad, key_span),
                            rows_of(value_tan_pad, key_span), allowed)

    block_outs = lax.map(one_block, jnp.arange(length // block_len, dtype=jnp.int32))

    def lay_out(stacked):
        return jnp.moveaxis(stacked, 0, 1).reshape(seq_count, length, full_width)

    return lay_out(block_outs[0]), lay_out(block_outs[1])


def reference(queries, keys, values, query_tan, key_tan, value_tan, weight_out, gate, gate_tan, cotangent):
    attended, attended_tan = windowed_attention(queries, keys, values, query_tan, key_tan, value_tan)
    full_width = attended.shape[2]
    weight_low = weight_out.astype(jnp.bfloat16)
    flat_att = attended.reshape(-1, full_width)
    projection = jnp.dot(flat_att, weight_low, preferred_element_type=jnp.float32).reshape(SEQS, LEN, D)
    projection_tan = jnp.dot(attended_tan.reshape(-1, full_width), weight_low, preferred_element_type=jnp.float32).reshape(SEQS, LEN, D)
    gate_rows = gate[:, None, :]
    mixed = (gate_rows * projection).astype(jnp.bfloat16)
    mixed_tan = (gate_tan[:, None, :] * projection + gate_rows * projection_tan).astype(jnp.bfloat16)
    weighted = (gate_rows * cotangent.astype(jnp.float32)).astype(jnp.bfloat16)
    weight_grad = lax.dot_general(flat_att, weighted.reshape(-1, D), (((0,), (0,)), ((), ())), preferred_element_type=jnp.float32)
    return mixed, mixed_tan, weight_grad
```

```python
import functools

import jax
import jax.numpy as jnp
from jax import lax
from jax.experimental import pallas as pl
from jax.experimental.pallas import tpu as pltpu
from jax.sharding import PartitionSpec as P

AXES = ("seq", "uly")
NX, NZ, NYL, NYH, NC = 4, 8, 2, 4, 2
HD = 128
PAIR = 2 * HD
NJ = 4
GROUP = NJ * PAIR
SCALE = HD ** (-0.5)
BF = jnp.bfloat16
F32 = jnp.float32


def device_of(x, yl, yh, z, c):
    return ((yl * NZ + z) * NX + x) * (NYH * NC) + yh * NC + c


def all_places():
    for x in range(NX):
        for yl in range(NYL):
            for yh in range(NYH):
                for z in range(NZ):
                    for c in range(NC):
                        yield x, yl, yh, z, c


def moves(rule):
    return sorted((device_of(*p), device_of(*rule(*p))) for p in all_places())


SWAP_CORE = moves(lambda x, yl, yh, z, c: (x, yl, yh, z, 1 - c))
SWAP_YLO = moves(lambda x, yl, yh, z, c: (x, 1 - yl, yh, z, c))
TURN = moves(lambda x, yl, yh, z, c: (yh, yl, x, z, c))


def swap_z(bit):
    return moves(lambda x, yl, yh, z, c: (x, yl, yh, z ^ bit, c))


def shift_x(by):
    return moves(lambda x, yl, yh, z, c: ((x + by) % NX, yl, yh, z, c))


COUNT = NX * NYL * NYH * NZ * NC
TO_NEXT = [(d, d + NC) for d in range(COUNT - NC)]
TO_PREV = [(d + NC, d) for d in range(COUNT - NC)]
GROUPS_X = [
    [device_of(x, yl, yh, z, c) for x in range(NX)]
    for yl in range(NYL) for yh in range(NYH) for z in range(NZ) for c in range(NC)
]
GROUPS_Z = [
    [device_of(x, yl, yh, z, c) for z in range(NZ)]
    for yl in range(NYL) for yh in range(NYH) for x in range(NX) for c in range(NC)
]
GROUPS_Y = [
    [device_of(x, yl, yh, z, c) for yl in range(NYL) for yh in range(NYH)]
    for z in range(NZ) for x in range(NX) for c in range(NC)
]


def send(array, pairs):
    return lax.ppermute(array, AXES, pairs)


def nt(left, right):
    return lax.dot_general(left, right, (((1,), (1,)), ((), ())), preferred_element_type=F32)


def nn(left, right):
    return lax.dot_general(left, right, (((1,), (0,)), ((), ())), preferred_element_type=F32)


def vmem_spec():
    return pl.BlockSpec(memory_space=pltpu.VMEM)


def smem_spec():
    return pl.BlockSpec(memory_space=pltpu.SMEM)


def params(*semantics):
    return pltpu.CompilerParams(
        vmem_limit_bytes=40 * 2**20, dimension_semantics=semantics or None
    )


def cost(flops, nbytes, trans=0):
    return pl.CostEstimate(flops=flops, bytes_accessed=nbytes, transcendentals=trans)


def group_cols(ref, s, j, side):
    return ref[s, :, pl.ds(pl.multiple_of(j * 2 * PAIR + side * PAIR, PAIR), PAIR)]


def split_body(meta, *refs, count, with_own):
    core = meta[0]
    ins, outs = refs[:count], refs[count:]
    for a in range(count):
        for s in range(2):
            for j in range(NJ):
                cols = slice(j * PAIR, (j + 1) * PAIR)
                if with_own:
                    outs[1][a, s, :, cols] = group_cols(ins[a], s, j, core)
                outs[0][a, s, :, cols] = group_cols(ins[a], s, j, 1 - core)


def split_groups(meta, arrays, with_own):
    count = len(arrays)
    seqs, rows, _ = arrays[0].shape
    shape = jax.ShapeDtypeStruct((count, seqs, rows, GROUP), BF)
    outs = [shape, shape] if with_own else [shape]
    return pl.pallas_call(
        functools.partial(split_body, count=count, with_own=with_own),
        out_shape=outs,
        in_specs=[smem_spec()] + [vmem_spec()] * count,
        out_specs=[vmem_spec()] * len(outs),
        compiler_params=params(),
        cost_estimate=cost(0, count * 2**20),
    )(meta, *arrays)


def join_body(meta, kt, vt, got, first, second):
    core = meta[0]
    rows = kt.shape[1]
    for a, ref in enumerate((kt, vt)):
        for s in range(2):
            for j in range(NJ):
                out = first if j < NJ // 2 else second
                cols = slice((j % 2) * PAIR, (j % 2 + 1) * PAIR)
                out[a, s, :rows, cols] = group_cols(ref, s, j, core)
                out[a, s, rows:, cols] = got[2 + a, s, :, j * PAIR : (j + 1) * PAIR]


def join_rows(meta, kt, vt, got):
    seqs, rows, _ = kt.shape
    shape = jax.ShapeDtypeStruct((2, seqs, 2 * rows, GROUP // 2), BF)
    return pl.pallas_call(
        join_body,
        out_shape=[shape, shape],
        in_specs=[smem_spec()] + [vmem_spec()] * 3,
        out_specs=[vmem_spec()] * 2,
        compiler_params=params(),
        cost_estimate=cost(0, 3 * 2**20),
    )(meta, kt, vt, got)


def allowed_keys(meta):
    core, chunk = meta[0], meta[1]
    span = 2 * 64
    shape = (span, 3 * span)
    rows = lax.broadcasted_iota(jnp.int32, shape, 0)
    cols = lax.broadcasted_iota(jnp.int32, shape, 1)
    q_pos = (rows + 64 * core) & (span - 1)
    k_pos = (cols + 64 * core) & (span - 1)
    block = cols >> 7
    before = (block == 0) & (k_pos >= q_pos) & (chunk > 0)
    after = (block == 2) & (k_pos <= q_pos) & (chunk < COUNT // NC - 1)
    return before | (block == 1) | after


def probs_of(q, k, mask):
    scores = jnp.where(mask, nt(q, k) * SCALE, -1e30)
    top = jnp.max(scores, axis=-1, keepdims=True)
    terms = jnp.exp(scores - top)
    return terms / jnp.sum(terms, axis=-1, keepdims=True)


def rows_of(refs, a, cols):
    return jnp.concatenate([ref[a, 0, :, cols] for ref in refs], axis=0)


def attend_body(meta, q_own, q_sib, lo, ls, mo, ms, ro, rs, quarter, out_own, out_sib):
    mask = allowed_keys(meta)
    keyed = (lo, ls, mo, ms, ro, rs)
    half = q_own.shape[1]
    for n in range(2):
        cols = slice(n * HD, (n + 1) * HD)
        q = jnp.concatenate([q_own[0, :, cols], q_sib[0, 0, :, cols]], axis=0)
        probs = probs_of(q, rows_of(keyed, 0, cols), mask).astype(BF)
        att = nn(probs, rows_of(keyed, 1, cols)).astype(BF)
        quarter[0, 0, 0, :, cols] = att[:half]
        quarter[0, 1, 0, :, cols] = att[half:]
        out_own[0, :, cols] = att[:half]
        out_sib[0, :, cols] = att[half:]


def attend(meta, queries, got, keyed):
    seqs, rows, _ = queries.shape
    pair = pl.BlockSpec((2, 1, rows, PAIR), lambda s, j, m: (0, s, 0, j))
    flat = pl.BlockSpec((1, rows, PAIR), lambda s, j, m: (s, 0, j))
    wide = jax.ShapeDtypeStruct((seqs, rows, GROUP), BF)
    return pl.pallas_call(
        attend_body,
        out_shape=[jax.ShapeDtypeStruct((NJ, 2, seqs, rows, PAIR), BF), wide, wide],
        grid_spec=pltpu.PrefetchScalarGridSpec(
            num_scalar_prefetch=1,
            grid=(seqs, NJ),
            in_specs=[
                pl.BlockSpec((1, rows, PAIR), lambda s, j, m: (s, 0, 2 * j + m[0])),
                pl.BlockSpec((1, 1, rows, PAIR), lambda s, j, m: (0, s, 0, j)),
            ]
            + [pair] * 6,
            out_specs=[
                pl.BlockSpec((1, 2, 1, rows, PAIR), lambda s, j, m: (j, 0, s, 0, 0)),
                flat,
                flat,
            ],
        ),
        compiler_params=params("arbitrary", "arbitrary"),
        cost_estimate=cost(2**29, 5 * 2**20, 2**20),
    )(meta, queries, got, *keyed)


def tangent_body(
    meta, q_own, q_sib, qt_own, qt_sib, lo, ls, mo, ms, ro, rs, lt, mt, rt, out_own, out_sib
):
    mask = allowed_keys(meta)
    keyed, keyed_tan = (lo, ls, mo, ms, ro, rs), (lt, mt, rt)
    half = q_own.shape[1]
    for n in range(2):
        cols = slice(n * HD, (n + 1) * HD)
        q = jnp.concatenate([q_own[0, :, cols], q_sib[0, 0, :, cols]], axis=0)
        qt = jnp.concatenate([qt_own[0, :, cols], qt_sib[0, 0, :, cols]], axis=0)
        k = rows_of(keyed, 0, cols)
        probs = probs_of(q, k, mask)
        tan = (nt(qt, k) + nt(q, rows_of(keyed_tan, 0, cols))) * SCALE
        probs_tan = probs * (tan - jnp.sum(probs * tan, axis=-1, keepdims=True))
        att = nn(probs_tan.astype(BF), rows_of(keyed, 1, cols)) + nn(
            probs.astype(BF), rows_of(keyed_tan, 1, cols)
        )
        att = att.astype(BF)
        out_own[0, :, cols] = att[:half]
        out_sib[0, :, cols] = att[half:]


def attend_tangent(meta, queries, query_tan, got, keyed, keyed_tan, part):
    seqs, rows, _ = queries.shape
    first = part * (NJ // 2)
    own = pl.BlockSpec((1, rows, PAIR), lambda s, j, m: (s, 0, 2 * (first + j) + m[0]))
    pair = pl.BlockSpec((2, 1, rows, PAIR), lambda s, j, m: (0, s, 0, first + j))
    tall = pl.BlockSpec((2, 1, 2 * rows, PAIR), lambda s, j, m: (0, s, 0, j))
    flat = pl.BlockSpec((1, rows, PAIR), lambda s, j, m: (s, 0, j))
    wide = jax.ShapeDtypeStruct((seqs, rows, GROUP // 2), BF)
    return pl.pallas_call(
        tangent_body,
        out_shape=[wide, wide],
        grid_spec=pltpu.PrefetchScalarGridSpec(
            num_scalar_prefetch=1,
            grid=(seqs, NJ // 2),
            in_specs=[
                own,
                pl.BlockSpec((1, 1, rows, PAIR), lambda s, j, m: (0, s, 0, first + j)),
                own,
                pl.BlockSpec((1, 1, rows, PAIR), lambda s, j, m: (1, s, 0, first + j)),
            ]
            + [pair] * 6
            + [tall] * 3,
            out_specs=[flat, flat],
        ),
        compiler_params=params("arbitrary", "arbitrary"),
        cost_estimate=cost(2**29, 5 * 2**20, 2**20),
    )(meta, queries, got, query_tan, got, *keyed, *keyed_tan)


def gate_rows(ref, rows):
    return jnp.concatenate(
        [jnp.broadcast_to(ref[s : s + 1, :], (rows, ref.shape[1])) for s in range(2)], axis=0
    )


def flat2(ref):
    return ref[...].reshape(ref.shape[0] * ref.shape[1], ref.shape[2])


def project_body(att_o, att_s, tan_o, tan_s, w_o, w_s, gate, gate_tan, mixed, part):
    rows = att_o.shape[1]
    half = tan_o.shape[2]
    proj = nt(flat2(att_o), w_o[...]) + nt(flat2(att_s), w_s[...])
    proj_tan = nt(flat2(tan_o), w_o[:, :half]) + nt(flat2(tan_s), w_s[:, :half])
    g, gt = gate_rows(gate, rows), gate_rows(gate_tan, rows)
    mixed[...] = (g * proj).astype(BF).reshape(mixed.shape)
    part[...] = (gt * proj + g * proj_tan).reshape(part.shape)


def project(att_o, att_s, tan_o, tan_s, w_o, w_s, gate, gate_tan):
    seqs, rows, _ = att_o.shape
    width = gate.shape[1]
    step = 512
    weight = pl.BlockSpec((step, GROUP), lambda i: (i, 0))
    gates = pl.BlockSpec((2, step), lambda i: (0, i))
    block = pl.BlockSpec((seqs, rows, step), lambda i: (0, 0, i))
    return pl.pallas_call(
        project_body,
        grid=(width // step,),
        out_shape=[
            jax.ShapeDtypeStruct((seqs, rows, width), BF),
            jax.ShapeDtypeStruct((seqs, rows, width), F32),
        ],
        in_specs=[vmem_spec()] * 4 + [weight, weight, gates, gates],
        out_specs=[block, block],
        compiler_params=params("arbitrary"),
        cost_estimate=cost(2**30, 9 * 2**20),
    )(att_o, att_s, tan_o, tan_s, w_o, w_s, gate, gate_tan)


def finish_body(tan_o, tan_s, w_o, w_s, gate, part, mixed_tan):
    rows = tan_o.shape[1]
    proj_tan = nt(flat2(tan_o), w_o[...]) + nt(flat2(tan_s), w_s[...])
    total = part[...].reshape(proj_tan.shape) + gate_rows(gate, rows) * proj_tan
    mixed_tan[...] = total.astype(BF).reshape(mixed_tan.shape)


def finish(tan_o, tan_s, w_o, w_s, gate, part):
    seqs, rows, width = part.shape
    step = 512
    weight = pl.BlockSpec((step, GROUP // 2), lambda i: (i, 1))
    block = pl.BlockSpec((seqs, rows, step), lambda i: (0, 0, i))
    return pl.pallas_call(
        finish_body,
        grid=(width // step,),
        out_shape=jax.ShapeDtypeStruct((seqs, rows, width), BF),
        in_specs=[vmem_spec()] * 2
        + [weight, weight, pl.BlockSpec((2, step), lambda i: (0, i)), block],
        out_specs=block,
        compiler_params=params("arbitrary"),
        cost_estimate=cost(2**29, 5 * 2**20),
    )(tan_o, tan_s, w_o, w_s, gate, part)


def grad_body(meta, w_own, w_sib, a0, a1, a2, a3, out):
    place = meta[2]
    total = None
    for back, att in enumerate((a0, a1, a2, a3)):
        origin = lax.rem(place + (NX - back), NX)
        for side, weighted in enumerate((w_own, w_sib)):
            block = att[side].reshape(-1, PAIR)
            term = nn(weighted[origin], block)
            total = term if total is None else total + term
    total = total.astype(BF)
    piece = out.shape[2]
    for yl in range(NYL):
        for z in range(NZ):
            start = (yl * NZ + z) * piece
            out[z, yl] = total[start : start + piece]


def grad_terms(meta, w_own, w_sib, parts):
    width = w_own.shape[1]
    return pl.pallas_call(
        grad_body,
        out_shape=jax.ShapeDtypeStruct((NZ, NYL, width // (NZ * NYL), PAIR), BF),
        in_specs=[smem_spec()] + [vmem_spec()] * 6,
        out_specs=vmem_spec(),
        compiler_params=params(),
        cost_estimate=cost(2**30, 4 * 2**20),
    )(meta, w_own, w_sib, *parts)


def in_order(mine, other, bit, axis):
    return jnp.where(
        bit == 0,
        jnp.concatenate([mine, other], axis=axis),
        jnp.concatenate([other, mine], axis=axis),
    )


def on_device(
    queries, keys, values, query_tan, key_tan, value_tan, weight_out, gate, gate_tan, cotangent
):
    seq_at, uly_at = lax.axis_index("seq"), lax.axis_index("uly")
    core = uly_at % NC
    x_at, z_at, yl_at = seq_at % NX, (seq_at // NX) % NZ, seq_at // (NX * NZ)
    chunk = seq_at * NYH + uly_at // NC
    meta = jnp.stack([core, chunk, x_at]).astype(jnp.int32)
    seqs, rows, _ = queries.shape

    kv_sib_out, kv_own = split_groups(meta, (keys, values), True)
    kv_lo, kv_ro = send(kv_own, TO_NEXT), send(kv_own, TO_PREV)
    kv_sib = send(kv_sib_out, SWAP_CORE)
    kv_ls, kv_rs = send(kv_sib, TO_NEXT), send(kv_sib, TO_PREV)

    (rest_out,) = split_groups(meta, (queries, query_tan, key_tan, value_tan), False)
    rest = send(rest_out, SWAP_CORE)
    tan_a, tan_b = join_rows(meta, key_tan, value_tan, rest)
    tan_a_l, tan_a_r = send(tan_a, TO_NEXT), send(tan_a, TO_PREV)
    tan_b_l, tan_b_r = send(tan_b, TO_NEXT), send(tan_b, TO_PREV)

    weighted = (gate[:, None, :] * cotangent.astype(F32)).astype(BF)
    weighted = weighted.reshape(seqs * rows, -1).T
    w_own = lax.all_gather(weighted, AXES, axis_index_groups=GROUPS_X)
    w_sib = send(w_own, SWAP_CORE)

    low = weight_out.astype(BF).reshape(NJ, NC, PAIR, -1)
    low = lax.dynamic_index_in_dim(low, core, 1, keepdims=False).reshape(GROUP, -1).T
    low = low.reshape(1, 1, -1, GROUP)
    low = in_order(low, send(low, SWAP_YLO), yl_at, 0)
    for step in range(3):
        bit = 1 << step
        low = in_order(low, send(low, swap_z(bit)), (z_at // bit) % 2, 1)
    low = low.reshape(NYL * NZ, -1, GROUP)
    proj_own = lax.all_gather(low, AXES, axis_index_groups=GROUPS_X, axis=1, tiled=True)
    proj_own = proj_own.reshape(-1, GROUP)
    proj_sib = send(proj_own, SWAP_CORE)

    keyed = (kv_lo, kv_ls, kv_own, kv_sib, kv_ro, kv_rs)
    quarter, att_own, att_out = attend(meta, queries, rest, keyed)
    parts = [lax.dynamic_index_in_dim(quarter, x_at, 0, keepdims=False)]
    for by in range(1, NX):
        piece = lax.dynamic_index_in_dim(quarter, (x_at + by) % NX, 0, keepdims=False)
        parts.append(send(piece, shift_x(by)))
    att_sib = send(att_out, SWAP_CORE)

    terms = grad_terms(meta, w_own, w_sib, parts)
    terms = lax.all_to_all(terms, AXES, 0, 0, axis_index_groups=GROUPS_Z, tiled=True)
    terms = jnp.sum(terms.astype(F32), axis=0).reshape(NYL * NYH, -1, PAIR)
    terms = lax.all_to_all(terms, AXES, 0, 0, axis_index_groups=GROUPS_Y, tiled=True)
    weight_grad = send(jnp.sum(terms, axis=0), TURN).T

    tan_own_a, tan_out_a = attend_tangent(
        meta, queries, query_tan, rest, keyed, (tan_a_l, tan_a, tan_a_r), 0
    )
    tan_sib_a = send(tan_out_a, SWAP_CORE)
    mixed, part = project(
        att_own, att_sib, tan_own_a, tan_sib_a, proj_own, proj_sib, gate, gate_tan
    )
    tan_own_b, tan_out_b = attend_tangent(
        meta, queries, query_tan, rest, keyed, (tan_b_l, tan_b, tan_b_r), 1
    )
    tan_sib_b = send(tan_out_b, SWAP_CORE)
    mixed_tan = finish(tan_own_b, tan_sib_b, proj_own, proj_sib, gate, part)
    return mixed, mixed_tan, weight_grad


def solution(mesh):
    rows = P(None, ("seq", "uly"), None)
    return jax.shard_map(
        on_device,
        mesh=mesh,
        in_specs=(rows,) * 6 + (P(None, "seq"), P(), P(), rows),
        out_specs=(rows, rows, P("uly", "seq")),
        check_vma=False,
    )
```

```python
import functools

import jax
import jax.numpy as jnp
from jax import lax
from jax.experimental import pallas as pl
from jax.experimental.pallas import tpu as pltpu
from jax.sharding import PartitionSpec as P

AXES = ("seq", "uly")
NX, NZ, NYL, NYH, NC = 4, 8, 2, 4, 2
HD = 128
PAIR = 2 * HD
NJ = 4
GROUP = NJ * PAIR
PIECES = ((0, 2), (2, 4))
SCALE = HD ** (-0.5)
BF = jnp.bfloat16
F32 = jnp.float32


def device_of(x, yl, yh, z, c):
    return ((yl * NZ + z) * NX + x) * (NYH * NC) + yh * NC + c


def all_places():
    for x in range(NX):
        for yl in range(NYL):
            for yh in range(NYH):
                for z in range(NZ):
                    for c in range(NC):
                        yield x, yl, yh, z, c


def moves(rule):
    return sorted((device_of(*p), device_of(*rule(*p))) for p in all_places())


SWAP_CORE = moves(lambda x, yl, yh, z, c: (x, yl, yh, z, 1 - c))
SWAP_YLO = moves(lambda x, yl, yh, z, c: (x, 1 - yl, yh, z, c))
TURN = moves(lambda x, yl, yh, z, c: (yh, yl, x, z, c))


def swap_z(bit):
    return moves(lambda x, yl, yh, z, c: (x, yl, yh, z ^ bit, c))


def shift_x(by):
    return moves(lambda x, yl, yh, z, c: ((x + by) % NX, yl, yh, z, c))


COUNT = NX * NYL * NYH * NZ * NC
TO_NEXT = [(d, d + NC) for d in range(COUNT - NC)]
TO_PREV = [(d + NC, d) for d in range(COUNT - NC)]
GROUPS_X = [
    [device_of(x, yl, yh, z, c) for x in range(NX)]
    for yl in range(NYL) for yh in range(NYH) for z in range(NZ) for c in range(NC)
]
GROUPS_Z = [
    [device_of(x, yl, yh, z, c) for z in range(NZ)]
    for yl in range(NYL) for yh in range(NYH) for x in range(NX) for c in range(NC)
]
GROUPS_ZYL = [
    [device_of(x, yl, yh, z, c) for yl in range(NYL) for z in range(NZ)]
    for yh in range(NYH) for x in range(NX) for c in range(NC)
]
GROUPS_Y = [
    [device_of(x, yl, yh, z, c) for yl in range(NYL) for yh in range(NYH)]
    for z in range(NZ) for x in range(NX) for c in range(NC)
]


def send(array, pairs, tag):
    with jax.named_scope(tag):
        return lax.ppermute(array, AXES, pairs)


def after(values):
    return lax.optimization_barrier(values)


def nt(left, right):
    return lax.dot_general(left, right, (((1,), (1,)), ((), ())), preferred_element_type=F32)


def nn(left, right):
    return lax.dot_general(left, right, (((1,), (0,)), ((), ())), preferred_element_type=F32)


def vmem_spec():
    return pl.BlockSpec(memory_space=pltpu.VMEM)


def smem_spec():
    return pl.BlockSpec(memory_space=pltpu.SMEM)


def params(*semantics):
    return pltpu.CompilerParams(
        vmem_limit_bytes=50 * 2**20, dimension_semantics=semantics or None
    )


def cost(flops, nbytes, trans=0):
    return pl.CostEstimate(flops=flops, bytes_accessed=nbytes, transcendentals=trans)


COSTS = dict(
    split=cost(1, 1),
    join=cost(1, 1),
    attend=cost(2**35, 1),
    tangent=cost(2**33, 1),
    project=cost(1, 1),
    finish=cost(1, 1),
    grad=cost(1, 1),
)


def group_cols(ref, s, j, side):
    return ref[s, :, pl.ds(pl.multiple_of(j * 2 * PAIR + side * PAIR, PAIR), PAIR)]


def split_body(meta, *refs):
    core = meta[0]
    ins, out = refs[:-1], refs[-1]
    for a, ref in enumerate(ins):
        for s in range(2):
            for j in range(NJ):
                out[a, s, :, j * PAIR : (j + 1) * PAIR] = group_cols(ref, s, j, 1 - core)


def split_groups(meta, arrays):
    count = len(arrays)
    seqs, rows, _ = arrays[0].shape
    return pl.pallas_call(
        split_body,
        out_shape=jax.ShapeDtypeStruct((count, seqs, rows, GROUP), BF),
        in_specs=[smem_spec()] + [vmem_spec()] * count,
        out_specs=vmem_spec(),
        compiler_params=params(),
        cost_estimate=COSTS["split"],
    )(meta, *arrays)


def join_body(meta, *refs, pieces, first):
    core = meta[0]
    count = len(refs) - 1 - len(pieces)
    ins, got, outs = refs[:count], refs[count], refs[count + 1 :]
    rows = ins[0].shape[1]
    for out, (sources, (start, stop)) in zip(outs, pieces):
        for n, a in enumerate(sources):
            for s in range(2):
                for j in range(start, stop):
                    cols = slice((j - start) * PAIR, (j - start + 1) * PAIR)
                    out[n, s, :rows, cols] = group_cols(ins[a], s, j, core)
                    out[n, s, rows:, cols] = got[first + a, s, :, j * PAIR : (j + 1) * PAIR]


def join_rows(meta, arrays, got, pieces, first):
    seqs, rows, _ = arrays[0].shape
    count = len(arrays)
    part = pl.BlockSpec((6, seqs, rows, GROUP), lambda: (0, 0, 0, 0))
    return pl.pallas_call(
        functools.partial(join_body, pieces=pieces, first=first),
        out_shape=[
            jax.ShapeDtypeStruct((len(src), seqs, 2 * rows, (stop - start) * PAIR), BF)
            for src, (start, stop) in pieces
        ],
        in_specs=[smem_spec()] + [vmem_spec()] * count + [part],
        out_specs=[vmem_spec()] * len(pieces),
        compiler_params=params(),
        cost_estimate=COSTS["join"],
    )(meta, *arrays, got)


def allowed_keys(meta):
    core, chunk = meta[0], meta[1]
    span = 2 * 64
    shape = (span, 3 * span)
    rows = lax.broadcasted_iota(jnp.int32, shape, 0)
    cols = lax.broadcasted_iota(jnp.int32, shape, 1)
    q_pos = (rows + 64 * core) & (span - 1)
    k_pos = (cols + 64 * core) & (span - 1)
    block = cols >> 7
    before = (block == 0) & (k_pos >= q_pos) & (chunk > 0)
    after = (block == 2) & (k_pos <= q_pos) & (chunk < COUNT // NC - 1)
    return before | (block == 1) | after


def probs_of(q, k, mask):
    scores = jnp.where(mask, nt(q, k) * SCALE, -1e30)
    top = jnp.max(scores, axis=-1, keepdims=True)
    terms = jnp.exp(scores - top)
    return terms / jnp.sum(terms, axis=-1, keepdims=True)


def rows_of(refs, a, cols):
    return jnp.concatenate([ref[a, 0, :, cols] for ref in refs], axis=0)


def attend_body(meta, q_ref, left, mid, right, quarter, wide):
    mask = allowed_keys(meta)
    keyed = (left, mid, right)
    for n in range(GROUP // HD):
        cols = slice(n * HD, (n + 1) * HD)
        probs = probs_of(q_ref[0, 0, :, cols], rows_of(keyed, 0, cols), mask).astype(BF)
        att = nn(probs, rows_of(keyed, 1, cols)).astype(BF)
        quarter[n // 2, 0, :, (n % 2) * HD : (n % 2 + 1) * HD] = att
        wide[0, :, cols] = att


def attend(meta, q_rows, keyed):
    _, seqs, rows, _ = q_rows.shape
    pair = pl.BlockSpec((2, 1, rows, GROUP), lambda s, m: (0, s, 0, 0))
    return pl.pallas_call(
        attend_body,
        out_shape=[
            jax.ShapeDtypeStruct((NJ, seqs, rows, PAIR), BF),
            jax.ShapeDtypeStruct((seqs, rows, GROUP), BF),
        ],
        grid_spec=pltpu.PrefetchScalarGridSpec(
            num_scalar_prefetch=1,
            grid=(seqs,),
            in_specs=[pl.BlockSpec((1, 1, rows, GROUP), lambda s, m: (0, s, 0, 0))] + [pair] * 3,
            out_specs=[
                pl.BlockSpec((NJ, 1, rows, PAIR), lambda s, m: (0, s, 0, 0)),
                pl.BlockSpec((1, rows, GROUP), lambda s, m: (s, 0, 0)),
            ],
        ),
        compiler_params=params("arbitrary"),
        cost_estimate=COSTS["attend"],
    )(meta, q_rows, *keyed)


def tangent_body(meta, q_ref, left, mid, right, left_tan, mid_tan, right_tan, wide):
    mask = allowed_keys(meta)
    keyed, keyed_tan = (left, mid, right), (left_tan, mid_tan, right_tan)
    for n in range(wide.shape[2] // HD):
        cols = slice(n * HD, (n + 1) * HD)
        q, qt = q_ref[0, 0, :, cols], q_ref[1, 0, :, cols]
        k = rows_of(keyed, 0, cols)
        probs = probs_of(q, k, mask)
        tan = (nt(qt, k) + nt(q, rows_of(keyed_tan, 0, cols))) * SCALE
        probs_tan = probs * (tan - jnp.sum(probs * tan, axis=-1, keepdims=True))
        att = nn(probs_tan.astype(BF), rows_of(keyed, 1, cols)) + nn(
            probs.astype(BF), rows_of(keyed_tan, 1, cols)
        )
        wide[0, :, cols] = att.astype(BF)


def attend_tangent(meta, q_rows, keyed, keyed_tan, piece):
    _, seqs, rows, _ = q_rows.shape
    first, stop = PIECES[piece]
    width = (stop - first) * PAIR
    part = pl.BlockSpec((2, 1, rows, width), lambda s, m: (0, s, 0, first * PAIR // width))
    tall = pl.BlockSpec((2, 1, rows, width), lambda s, m: (0, s, 0, 0))
    return pl.pallas_call(
        tangent_body,
        out_shape=jax.ShapeDtypeStruct((seqs, rows, width), BF),
        grid_spec=pltpu.PrefetchScalarGridSpec(
            num_scalar_prefetch=1,
            grid=(seqs,),
            in_specs=[part] * 4 + [tall] * 3,
            out_specs=pl.BlockSpec((1, rows, width), lambda s, m: (s, 0, 0)),
        ),
        compiler_params=params("arbitrary"),
        cost_estimate=COSTS["tangent"],
    )(meta, q_rows, *keyed, *keyed_tan)


def gate_rows(ref, rows):
    return jnp.concatenate(
        [jnp.broadcast_to(ref[s : s + 1, :], (rows, ref.shape[1])) for s in range(2)], axis=0
    )


def flat2(ref):
    return ref[...].reshape(ref.shape[0] * ref.shape[1], ref.shape[2])


def put_halves(value, here, other, at):
    rows = here.shape[-2]
    for s in range(2):
        here[at, s] = value[2 * s * rows : (2 * s + 1) * rows]
        other[at, s] = value[(2 * s + 1) * rows : (2 * s + 2) * rows]


def project_body(att, tan, weight, gate, gate_tan, here, other):
    rows = att.shape[1]
    proj = nt(flat2(att), weight[...])
    proj_tan = nt(flat2(tan), weight[:, : tan.shape[2]])
    g, gt = gate_rows(gate, rows), gate_rows(gate_tan, rows)
    put_halves(g * proj, here, other, 0)
    put_halves(gt * proj + g * proj_tan, here, other, 1)


def project(att, tan, weight, gate, gate_tan):
    seqs, rows, _ = att.shape
    width = gate.shape[1]
    step = 512
    gates = pl.BlockSpec((2, step), lambda i: (0, i))
    block = pl.BlockSpec((2, seqs, rows // 2, step), lambda i: (0, 0, 0, i))
    return pl.pallas_call(
        project_body,
        grid=(width // step,),
        out_shape=[jax.ShapeDtypeStruct((2, seqs, rows // 2, width), F32)] * 2,
        in_specs=[vmem_spec()] * 2
        + [pl.BlockSpec((step, GROUP), lambda i: (i, 0)), gates, gates],
        out_specs=[block, block],
        compiler_params=params("arbitrary"),
        cost_estimate=COSTS["project"],
    )(att, tan, weight, gate, gate_tan)


def finish_body(tan, weight, gate, here, other):
    proj_tan = nt(flat2(tan), weight[...])
    put_halves(gate_rows(gate, tan.shape[1]) * proj_tan, here, other, 0)


def finish(tan, weight, gate):
    seqs, rows, half = tan.shape
    width = gate.shape[1]
    step = 512
    block = pl.BlockSpec((1, seqs, rows // 2, step), lambda i: (0, 0, 0, i))
    return pl.pallas_call(
        finish_body,
        grid=(width // step,),
        out_shape=[jax.ShapeDtypeStruct((1, seqs, rows // 2, width), F32)] * 2,
        in_specs=[
            vmem_spec(),
            pl.BlockSpec((step, half), lambda i: (i, 1)),
            pl.BlockSpec((2, step), lambda i: (0, i)),
        ],
        out_specs=[block, block],
        compiler_params=params("arbitrary"),
        cost_estimate=COSTS["finish"],
    )(tan, weight, gate)


def grad_body(w_own, w_sib, att, out):
    half = att.shape[2] // 2
    total = None
    for x in range(NX):
        for side, weighted in enumerate((w_own, w_sib)):
            rows = slice(side * half, (side + 1) * half)
            block = jnp.concatenate([att[x, s, rows] for s in range(2)], axis=0)
            term = nn(weighted[x], block)
            total = term if total is None else total + term
    total = total.astype(BF)
    piece = out.shape[2]
    for yl in range(NYL):
        for z in range(NZ):
            start = (yl * NZ + z) * piece
            out[z, yl] = total[start : start + piece]


def grad_terms(w_own, w_sib, att):
    width = w_own.shape[1]
    return pl.pallas_call(
        grad_body,
        out_shape=jax.ShapeDtypeStruct((NZ, NYL, width // (NZ * NYL), PAIR), BF),
        in_specs=[vmem_spec()] * 3,
        out_specs=vmem_spec(),
        compiler_params=params(),
        cost_estimate=COSTS["grad"],
    )(w_own, w_sib, att)


def on_device(
    queries, keys, values, query_tan, key_tan, value_tan, weight_out, gate, gate_tan, cotangent
):
    seq_at, uly_at = lax.axis_index("seq"), lax.axis_index("uly")
    core = uly_at % NC
    chunk = seq_at * NYH + uly_at // NC
    meta = jnp.stack([core, chunk]).astype(jnp.int32)
    seqs, rows, _ = queries.shape

    arrays = (keys, values, queries, query_tan, key_tan, value_tan)
    got = send(split_groups(meta, arrays), SWAP_CORE, "Sx")
    (kv,) = join_rows(meta, arrays[:2], got, (((0, 1), (0, NJ)),), 0)
    keyed = (send(kv, TO_NEXT, "Ha"), kv, send(kv, TO_PREV, "Hb"))
    q_rows, *tans = join_rows(
        meta, arrays[2:], got, (((0, 1), (0, NJ)),) + tuple(((2, 3), p) for p in PIECES), 2
    )
    tans = [[send(t, TO_NEXT, "T%da" % n), t, send(t, TO_PREV, "T%db" % n)] for n, t in enumerate(tans)]

    weighted = (gate[:, None, :] * cotangent.astype(F32)).astype(BF)
    weighted = weighted.reshape(seqs * rows, -1).T
    w_own = lax.all_gather(weighted, AXES, axis_index_groups=GROUPS_X)
    w_own, _ = after((w_own, kv))
    w_sib = send(w_own, SWAP_CORE, "Cswap")

    low = weight_out.astype(BF).reshape(NJ, NC, PAIR, -1)
    low = lax.dynamic_index_in_dim(low, core, 1, keepdims=False).reshape(GROUP, -1).T
    low = jnp.broadcast_to(low[None], (NYL * NZ,) + low.shape)
    low = lax.all_to_all(low, AXES, 0, 0, axis_index_groups=GROUPS_ZYL, tiled=True)
    weight = lax.all_gather(low, AXES, axis_index_groups=GROUPS_X, axis=1, tiled=True)
    weight = weight.reshape(-1, GROUP)

    quarter, att = attend(meta, q_rows, keyed)
    quarter, _ = after((quarter, low))
    quarter = lax.all_to_all(quarter, AXES, 0, 0, axis_index_groups=GROUPS_X, tiled=True)
    (quarter, tans[0][0], tans[0][2]) = after((quarter, tans[0][0], tans[0][2]))
    terms = grad_terms(w_own, w_sib, quarter)
    terms = lax.all_to_all(terms, AXES, 0, 0, axis_index_groups=GROUPS_Z, tiled=True)
    terms = jnp.sum(terms.astype(F32), axis=0).reshape(NYL * NYH, -1, PAIR)
    terms = lax.all_to_all(terms, AXES, 0, 0, axis_index_groups=GROUPS_Y, tiled=True)
    weight_grad = send(jnp.sum(terms, axis=0), TURN, "Turn").T

    tan_first = attend_tangent(meta, q_rows, keyed, tans[0], 0)
    here, other = project(att, tan_first, weight, gate, gate_tan)
    other = send(other, SWAP_CORE, "Pswap")
    tan_last = attend_tangent(meta, q_rows, keyed, tans[1], 1)
    rest, rest_other = finish(tan_last, weight, gate)
    rest_other = send(rest_other, SWAP_CORE, "Uswap")
    mixed = (here[0] + other[0]).astype(BF)
    mixed_tan = ((here[1] + other[1]) + (rest[0] + rest_other[0])).astype(BF)
    return mixed, mixed_tan, weight_grad


def solution(mesh):
    rows = P(None, ("seq", "uly"), None)
    return jax.shard_map(
        on_device,
        mesh=mesh,
        in_specs=(rows,) * 6 + (P(None, "seq"), P(), P(), rows),
        out_specs=(rows, rows, P("uly", "seq")),
        check_vma=False,
    )
```

```python
import functools

import jax
import jax.numpy as jnp
from jax import lax
from jax.experimental import pallas as pl
from jax.experimental.pallas import tpu as pltpu
from jax.sharding import PartitionSpec as P

AXES = ("seq", "uly")
NX, NZ, NYL, NYH, NC = 4, 8, 2, 4, 2
HD = 128
PAIR = 2 * HD
NJ = 4
GROUP = NJ * PAIR
PIECES = ((0, 2), (2, 4))
SCALE = HD ** (-0.5)
LOG2E = 1.4426950408889634
BF = jnp.bfloat16
F32 = jnp.float32


def device_of(x, yl, yh, z, c):
    return ((yl * NZ + z) * NX + x) * (NYH * NC) + yh * NC + c


def all_places():
    for x in range(NX):
        for yl in range(NYL):
            for yh in range(NYH):
                for z in range(NZ):
                    for c in range(NC):
                        yield x, yl, yh, z, c


def moves(rule):
    return sorted((device_of(*p), device_of(*rule(*p))) for p in all_places())


SWAP_CORE = moves(lambda x, yl, yh, z, c: (x, yl, yh, z, 1 - c))
SWAP_YLO = moves(lambda x, yl, yh, z, c: (x, 1 - yl, yh, z, c))
TURN = moves(lambda x, yl, yh, z, c: (yh, yl, x, z, c))


def swap_z(bit):
    return moves(lambda x, yl, yh, z, c: (x, yl, yh, z ^ bit, c))


def shift_x(by):
    return moves(lambda x, yl, yh, z, c: ((x + by) % NX, yl, yh, z, c))


COUNT = NX * NYL * NYH * NZ * NC
TO_NEXT = [(d, d + NC) for d in range(COUNT - NC)]
TO_PREV = [(d + NC, d) for d in range(COUNT - NC)]
GROUPS_X = [
    [device_of(x, yl, yh, z, c) for x in range(NX)]
    for yl in range(NYL) for yh in range(NYH) for z in range(NZ) for c in range(NC)
]
GROUPS_Z = [
    [device_of(x, yl, yh, z, c) for z in range(NZ)]
    for yl in range(NYL) for yh in range(NYH) for x in range(NX) for c in range(NC)
]
GROUPS_XYL = [
    [device_of(x, yl, yh, z, c) for yl in range(NYL) for x in range(NX)]
    for yh in range(NYH) for z in range(NZ) for c in range(NC)
]
GROUPS_Y = [
    [device_of(x, yl, yh, z, c) for yl in range(NYL) for yh in range(NYH)]
    for z in range(NZ) for x in range(NX) for c in range(NC)
]


def send(array, pairs, tag):
    with jax.named_scope(tag):
        return lax.ppermute(array, AXES, pairs)


def after(values):
    return lax.optimization_barrier(values)


def nt(left, right):
    return lax.dot_general(left, right, (((1,), (1,)), ((), ())), preferred_element_type=F32)


def nn(left, right):
    return lax.dot_general(left, right, (((1,), (0,)), ((), ())), preferred_element_type=F32)


def vmem_spec():
    return pl.BlockSpec(memory_space=pltpu.VMEM)


def smem_spec():
    return pl.BlockSpec(memory_space=pltpu.SMEM)


def params(*semantics):
    return pltpu.CompilerParams(
        vmem_limit_bytes=60 * 2**20, dimension_semantics=semantics or None
    )


def cost(flops, nbytes, trans=0):
    return pl.CostEstimate(flops=flops, bytes_accessed=nbytes, transcendentals=trans)


COSTS = dict(
    split=cost(1, 1),
    join=cost(1, 1),
    attend=cost(2**37, 1),
    tangent=cost(2**33, 1),
    project=cost(2**33, 1),
    finish=cost(2**33, 1),
    grad=cost(1, 1),
)


def group_cols(ref, s, j, side):
    return ref[s, :, pl.ds(pl.multiple_of(j * 2 * PAIR + side * PAIR, PAIR), PAIR)]


def split_body(meta, *refs):
    core = meta[0]
    ins, out = refs[:-1], refs[-1]
    for a, ref in enumerate(ins):
        for s in range(2):
            for j in range(NJ):
                out[a, s, :, j * PAIR : (j + 1) * PAIR] = group_cols(ref, s, j, 1 - core)


def split_groups(meta, arrays):
    count = len(arrays)
    seqs, rows, _ = arrays[0].shape
    return pl.pallas_call(
        split_body,
        out_shape=jax.ShapeDtypeStruct((count, seqs, rows, GROUP), BF),
        in_specs=[smem_spec()] + [vmem_spec()] * count,
        out_specs=vmem_spec(),
        compiler_params=params(),
        cost_estimate=COSTS["split"],
    )(meta, *arrays)


def join_body(meta, *refs, pieces, first):
    core = meta[0]
    count = len(refs) - 1 - len(pieces)
    ins, got, outs = refs[:count], refs[count], refs[count + 1 :]
    rows = ins[0].shape[1]
    for out, (sources, (start, stop)) in zip(outs, pieces):
        for n, a in enumerate(sources):
            for s in range(2):
                for j in range(start, stop):
                    cols = slice((j - start) * PAIR, (j - start + 1) * PAIR)
                    out[n, s, :rows, cols] = group_cols(ins[a], s, j, core)
                    out[n, s, rows:, cols] = got[first + a, s, :, j * PAIR : (j + 1) * PAIR]


def join_rows(meta, arrays, got, pieces, first):
    seqs, rows, _ = arrays[0].shape
    count = len(arrays)
    part = pl.BlockSpec((6, seqs, rows, GROUP), lambda: (0, 0, 0, 0))
    return pl.pallas_call(
        functools.partial(join_body, pieces=pieces, first=first),
        out_shape=[
            jax.ShapeDtypeStruct((len(src), seqs, 2 * rows, (stop - start) * PAIR), BF)
            for src, (start, stop) in pieces
        ],
        in_specs=[smem_spec()] + [vmem_spec()] * count + [part],
        out_specs=[vmem_spec()] * len(pieces),
        compiler_params=params(),
        cost_estimate=COSTS["join"],
    )(meta, *arrays, got)


def key_bias(meta):
    core, chunk = meta[0], meta[1]
    span = 2 * 64
    rows = lax.broadcasted_iota(jnp.int32, (span, span), 0)
    cols = lax.broadcasted_iota(jnp.int32, (span, span), 1)
    q_pos = (rows + 64 * core) & (span - 1)
    k_pos = (cols + 64 * core) & (span - 1)
    before = (k_pos >= q_pos) & (chunk > 0)
    after_ = (k_pos <= q_pos) & (chunk < COUNT // NC - 1)
    return jnp.where(before, 0.0, -1e30), jnp.where(after_, 0.0, -1e30)


def exp_terms(q, keys, bias):
    scores = [nt(q, k) for k in keys]
    scores = [scores[0] + bias[0], scores[1], scores[2] + bias[1]]
    top = jnp.maximum(jnp.maximum(scores[0], scores[1]), scores[2])
    top = jnp.max(top, axis=-1, keepdims=True)
    terms = [jnp.exp2((score - top) * (SCALE * LOG2E)) for score in scores]
    return terms, 1.0 / jnp.sum(terms[0] + terms[1] + terms[2], axis=-1, keepdims=True)


def added(terms):
    return terms[0] + terms[1] + terms[2]


def blocks_of(refs, a, cols):
    return [ref[a, 0, :, cols] for ref in refs]


def attend_body(meta, q_ref, left, mid, right, quarter, wide):
    bias = key_bias(meta)
    keyed = (left, mid, right)
    for n in range(GROUP // HD):
        cols = slice(n * HD, (n + 1) * HD)
        terms, inverse = exp_terms(q_ref[0, 0, :, cols], blocks_of(keyed, 0, cols), bias)
        values = blocks_of(keyed, 1, cols)
        att = added([nn((t * inverse).astype(BF), v) for t, v in zip(terms, values)]).astype(BF)
        quarter[n // 2, 0, :, (n % 2) * HD : (n % 2 + 1) * HD] = att
        wide[0, :, cols] = att


def attend(meta, q_rows, keyed):
    _, seqs, rows, _ = q_rows.shape
    pair = pl.BlockSpec((2, 1, rows, GROUP), lambda s, m: (0, s, 0, 0))
    return pl.pallas_call(
        attend_body,
        out_shape=[
            jax.ShapeDtypeStruct((NJ, seqs, rows, PAIR), BF),
            jax.ShapeDtypeStruct((seqs, rows, GROUP), BF),
        ],
        grid_spec=pltpu.PrefetchScalarGridSpec(
            num_scalar_prefetch=1,
            grid=(seqs,),
            in_specs=[pl.BlockSpec((1, 1, rows, GROUP), lambda s, m: (0, s, 0, 0))] + [pair] * 3,
            out_specs=[
                pl.BlockSpec((NJ, 1, rows, PAIR), lambda s, m: (0, s, 0, 0)),
                pl.BlockSpec((1, rows, GROUP), lambda s, m: (s, 0, 0)),
            ],
        ),
        compiler_params=params("arbitrary"),
        cost_estimate=COSTS["attend"],
    )(meta, q_rows, *keyed)


def tangent_body(meta, q_ref, left, mid, right, left_tan, mid_tan, right_tan, wide):
    bias = key_bias(meta)
    keyed, keyed_tan = (left, mid, right), (left_tan, mid_tan, right_tan)
    for n in range(wide.shape[2] // HD):
        cols = slice(n * HD, (n + 1) * HD)
        q, qt = q_ref[0, 0, :, cols], q_ref[1, 0, :, cols]
        keys = blocks_of(keyed, 0, cols)
        terms, inverse = exp_terms(q, keys, bias)
        probs = [t * inverse for t in terms]
        tans = [
            (nt(qt, k) + nt(q, kt)) * SCALE
            for k, kt in zip(keys, blocks_of(keyed_tan, 0, cols))
        ]
        mean = jnp.sum(added([p * t for p, t in zip(probs, tans)]), axis=-1, keepdims=True)
        att = added([nn(p.astype(BF), v) for p, v in zip(probs, blocks_of(keyed_tan, 1, cols))])
        probs = [p * (t - mean) for p, t in zip(probs, tans)]
        att += added([nn(p.astype(BF), v) for p, v in zip(probs, blocks_of(keyed, 1, cols))])
        wide[0, :, cols] = att.astype(BF)


def attend_tangent(meta, q_rows, keyed, keyed_tan, piece):
    _, seqs, rows, _ = q_rows.shape
    first, stop = PIECES[piece]
    width = (stop - first) * PAIR
    part = pl.BlockSpec((2, 1, rows, width), lambda s, m: (0, s, 0, first * PAIR // width))
    tall = pl.BlockSpec((2, 1, rows, width), lambda s, m: (0, s, 0, 0))
    return pl.pallas_call(
        tangent_body,
        out_shape=jax.ShapeDtypeStruct((seqs, rows, width), BF),
        grid_spec=pltpu.PrefetchScalarGridSpec(
            num_scalar_prefetch=1,
            grid=(seqs,),
            in_specs=[part] * 4 + [tall] * 3,
            out_specs=pl.BlockSpec((1, rows, width), lambda s, m: (s, 0, 0)),
        ),
        compiler_params=params("arbitrary"),
        cost_estimate=COSTS["tangent"],
    )(meta, q_rows, *keyed, *keyed_tan)


def gate_rows(ref, rows):
    return jnp.concatenate(
        [jnp.broadcast_to(ref[s : s + 1, :], (rows, ref.shape[1])) for s in range(2)], axis=0
    )


def flat2(ref):
    return ref[...].reshape(ref.shape[0] * ref.shape[1], ref.shape[2])


def put_halves(value, here, other, at):
    rows = here.shape[-2]
    for s in range(2):
        here[at, s] = value[2 * s * rows : (2 * s + 1) * rows]
        other[at, s] = value[(2 * s + 1) * rows : (2 * s + 2) * rows]


def project_body(att, tan, weight, gate, gate_tan, here, other):
    rows = att.shape[1]
    proj = nt(flat2(att), weight[...])
    proj_tan = nt(flat2(tan), weight[:, : tan.shape[2]])
    g, gt = gate_rows(gate, rows), gate_rows(gate_tan, rows)
    put_halves(g * proj, here, other, 0)
    put_halves(gt * proj + g * proj_tan, here, other, 1)


def project(att, tan, weight, gate, gate_tan):
    seqs, rows, _ = att.shape
    width = gate.shape[1]
    step = 512
    gates = pl.BlockSpec((2, step), lambda i: (0, i))
    block = pl.BlockSpec((2, seqs, rows // 2, step), lambda i: (0, 0, 0, i))
    return pl.pallas_call(
        project_body,
        grid=(width // step,),
        out_shape=[jax.ShapeDtypeStruct((2, seqs, rows // 2, width), F32)] * 2,
        in_specs=[vmem_spec()] * 2
        + [pl.BlockSpec((step, GROUP), lambda i: (i, 0)), gates, gates],
        out_specs=[block, block],
        compiler_params=params("arbitrary"),
        cost_estimate=COSTS["project"],
    )(att, tan, weight, gate, gate_tan)


def finish_body(tan, weight, gate, here, other):
    proj_tan = nt(flat2(tan), weight[...])
    put_halves(gate_rows(gate, tan.shape[1]) * proj_tan, here, other, 0)


def finish(tan, weight, gate):
    seqs, rows, half = tan.shape
    width = gate.shape[1]
    step = 512
    block = pl.BlockSpec((1, seqs, rows // 2, step), lambda i: (0, 0, 0, i))
    return pl.pallas_call(
        finish_body,
        grid=(width // step,),
        out_shape=[jax.ShapeDtypeStruct((1, seqs, rows // 2, width), F32)] * 2,
        in_specs=[
            vmem_spec(),
            pl.BlockSpec((step, half), lambda i: (i, 1)),
            pl.BlockSpec((2, step), lambda i: (0, i)),
        ],
        out_specs=[block, block],
        compiler_params=params("arbitrary"),
        cost_estimate=COSTS["finish"],
    )(tan, weight, gate)


def grad_body(w_own, w_sib, att, out):
    half = att.shape[2] // 2
    total = None
    for x in range(NX):
        for side, weighted in enumerate((w_own, w_sib)):
            rows = slice(side * half, (side + 1) * half)
            block = jnp.concatenate([att[x, s, rows] for s in range(2)], axis=0)
            term = nn(weighted[x], block)
            total = term if total is None else total + term
    total = total.astype(BF)
    piece = out.shape[2]
    for yl in range(NYL):
        for z in range(NZ):
            start = (yl * NZ + z) * piece
            out[z, yl] = total[start : start + piece]


def grad_terms(w_own, w_sib, att):
    width = w_own.shape[1]
    return pl.pallas_call(
        grad_body,
        out_shape=jax.ShapeDtypeStruct((NZ, NYL, width // (NZ * NYL), PAIR), BF),
        in_specs=[vmem_spec()] * 3,
        out_specs=vmem_spec(),
        compiler_params=params(),
        cost_estimate=COSTS["grad"],
    )(w_own, w_sib, att)


def on_device(
    queries, keys, values, query_tan, key_tan, value_tan, weight_out, gate, gate_tan, cotangent
):
    seq_at, uly_at = lax.axis_index("seq"), lax.axis_index("uly")
    core = uly_at % NC
    chunk = seq_at * NYH + uly_at // NC
    meta = jnp.stack([core, chunk]).astype(jnp.int32)
    seqs, rows, _ = queries.shape

    arrays = (keys, values, queries, query_tan, key_tan, value_tan)
    got = send(split_groups(meta, arrays), SWAP_CORE, "Sx")
    (kv,) = join_rows(meta, arrays[:2], got, (((0, 1), (0, NJ)),), 0)
    keyed = (send(kv, TO_NEXT, "Ha"), kv, send(kv, TO_PREV, "Hb"))
    q_rows, *tans = join_rows(
        meta, arrays[2:], got, (((0, 1), (0, NJ)),) + tuple(((2, 3), p) for p in PIECES), 2
    )
    tans = [[send(t, TO_NEXT, "T%da" % n), t, send(t, TO_PREV, "T%db" % n)] for n, t in enumerate(tans)]

    cotangent, _ = after((cotangent, got))
    weighted = (gate[:, None, :] * cotangent.astype(F32)).astype(BF)
    weighted = weighted.reshape(seqs * rows, -1).T
    w_own = lax.all_gather(weighted, AXES, axis_index_groups=GROUPS_X)
    w_own, _ = after((w_own, kv))
    w_sib = send(w_own, SWAP_CORE, "Cswap")

    low = weight_out.astype(BF).reshape(NJ, NC, PAIR, -1)
    low = lax.dynamic_index_in_dim(low, core, 1, keepdims=False).reshape(GROUP, -1).T
    low = jnp.broadcast_to(low[None], (NYL * NX,) + low.shape)
    low = lax.all_to_all(low, AXES, 0, 0, axis_index_groups=GROUPS_XYL, tiled=True)
    low = low.reshape(NYL, -1, GROUP)
    weight = lax.all_gather(low, AXES, axis_index_groups=GROUPS_Z, axis=1, tiled=True)
    weight = weight.reshape(-1, GROUP)

    quarter, att = attend(meta, q_rows, keyed)
    quarter, _ = after((quarter, low))
    quarter = lax.all_to_all(quarter, AXES, 0, 0, axis_index_groups=GROUPS_X, tiled=True)
    (quarter, tans[1][0], tans[1][2]) = after((quarter, tans[1][0], tans[1][2]))
    terms = grad_terms(w_own, w_sib, quarter)
    terms = lax.all_to_all(terms, AXES, 0, 0, axis_index_groups=GROUPS_Z, tiled=True)
    terms = jnp.sum(terms.astype(F32), axis=0).reshape(NYL * NYH, -1, PAIR)
    summed = terms
    terms = lax.all_to_all(terms, AXES, 0, 0, axis_index_groups=GROUPS_Y, tiled=True)
    terms = jnp.sum(terms, axis=0)
    weight_grad = send(terms, TURN, "Turn").T

    tan_first = attend_tangent(meta, q_rows, keyed, tans[0], 0)
    att, _ = after((att, summed))
    here, other = project(att, tan_first, weight, gate, gate_tan)
    other = send(other, SWAP_CORE, "Pswap")
    tan_last = attend_tangent(meta, q_rows, keyed, tans[1], 1)
    tan_last, _ = after((tan_last, terms))
    rest, rest_other = finish(tan_last, weight, gate)
    rest_other = send(rest_other, SWAP_CORE, "Uswap")
    mixed = (here[0] + other[0]).astype(BF)
    mixed_tan = ((here[1] + other[1]) + (rest[0] + rest_other[0])).astype(BF)
    return mixed, mixed_tan, weight_grad


def solution(mesh):
    rows = P(None, ("seq", "uly"), None)
    return jax.shard_map(
        on_device,
        mesh=mesh,
        in_specs=(rows,) * 6 + (P(None, "seq"), P(), P(), rows),
        out_specs=(rows, rows, P("uly", "seq")),
        check_vma=False,
    )
```

```python
import functools

import jax
import jax.numpy as jnp
from jax import lax
from jax.experimental import pallas as pl
from jax.experimental.pallas import tpu as pltpu
from jax.sharding import PartitionSpec as P

AXES = ("seq", "uly")
NX, NZ, NYL, NYH, NC = 4, 8, 2, 4, 2
HD = 128
PAIR = 2 * HD
NJ = 4
GROUP = NJ * PAIR
PIECES = ((0, 2), (2, 4))
SCALE = HD ** (-0.5)
LOG2E = 1.4426950408889634
BF = jnp.bfloat16
F32 = jnp.float32


def device_of(x, yl, yh, z, c):
    return ((yl * NZ + z) * NX + x) * (NYH * NC) + yh * NC + c


def all_places():
    for x in range(NX):
        for yl in range(NYL):
            for yh in range(NYH):
                for z in range(NZ):
                    for c in range(NC):
                        yield x, yl, yh, z, c


def moves(rule):
    return sorted((device_of(*p), device_of(*rule(*p))) for p in all_places())


SWAP_CORE = moves(lambda x, yl, yh, z, c: (x, yl, yh, z, 1 - c))
SWAP_YLO = moves(lambda x, yl, yh, z, c: (x, 1 - yl, yh, z, c))
TURN = moves(lambda x, yl, yh, z, c: (yh, yl, x, z, c))


def swap_z(bit):
    return moves(lambda x, yl, yh, z, c: (x, yl, yh, z ^ bit, c))


def shift_x(by):
    return moves(lambda x, yl, yh, z, c: ((x + by) % NX, yl, yh, z, c))


COUNT = NX * NYL * NYH * NZ * NC
TO_NEXT = [(d, d + NC) for d in range(COUNT - NC)]
TO_PREV = [(d + NC, d) for d in range(COUNT - NC)]
GROUPS_X = [
    [device_of(x, yl, yh, z, c) for x in range(NX)]
    for yl in range(NYL) for yh in range(NYH) for z in range(NZ) for c in range(NC)
]
GROUPS_Z = [
    [device_of(x, yl, yh, z, c) for z in range(NZ)]
    for yl in range(NYL) for yh in range(NYH) for x in range(NX) for c in range(NC)
]
GROUPS_Y = [
    [device_of(x, yl, yh, z, c) for yl in range(NYL) for yh in range(NYH)]
    for z in range(NZ) for x in range(NX) for c in range(NC)
]


def send(array, pairs, tag):
    with jax.named_scope(tag):
        return lax.ppermute(array, AXES, pairs)


def after(values):
    return lax.optimization_barrier(values)


def nt(left, right):
    return lax.dot_general(left, right, (((1,), (1,)), ((), ())), preferred_element_type=F32)


def nn(left, right):
    return lax.dot_general(left, right, (((1,), (0,)), ((), ())), preferred_element_type=F32)


def vmem_spec():
    return pl.BlockSpec(memory_space=pltpu.VMEM)


def smem_spec():
    return pl.BlockSpec(memory_space=pltpu.SMEM)


def params(*semantics):
    return pltpu.CompilerParams(
        vmem_limit_bytes=60 * 2**20, dimension_semantics=semantics or None
    )


def cost(flops, nbytes, trans=0):
    return pl.CostEstimate(flops=flops, bytes_accessed=nbytes, transcendentals=trans)


COSTS = dict(
    split=cost(1, 1),
    join=cost(1, 1),
    attend=cost(2**37, 1),
    tangent=cost(2**33, 1),
    project=cost(2**33, 1),
    finish=cost(2**33, 1),
    grad=cost(1, 1),
)


def group_cols(ref, s, j, side):
    return ref[s, :, pl.ds(pl.multiple_of(j * 2 * PAIR + side * PAIR, PAIR), PAIR)]


def split_body(meta, *refs):
    core = meta[0]
    ins, out = refs[:-1], refs[-1]
    for a, ref in enumerate(ins):
        for s in range(2):
            for j in range(NJ):
                out[a, s, :, j * PAIR : (j + 1) * PAIR] = group_cols(ref, s, j, 1 - core)


def split_groups(meta, arrays):
    count = len(arrays)
    seqs, rows, _ = arrays[0].shape
    return pl.pallas_call(
        split_body,
        out_shape=jax.ShapeDtypeStruct((count, seqs, rows, GROUP), BF),
        in_specs=[smem_spec()] + [vmem_spec()] * count,
        out_specs=vmem_spec(),
        compiler_params=params(),
        cost_estimate=COSTS["split"],
    )(meta, *arrays)


def join_body(meta, *refs, pieces, first):
    core = meta[0]
    count = len(refs) - 1 - len(pieces)
    ins, got, outs = refs[:count], refs[count], refs[count + 1 :]
    rows = ins[0].shape[1]
    for out, (sources, (start, stop)) in zip(outs, pieces):
        for n, a in enumerate(sources):
            for s in range(2):
                for j in range(start, stop):
                    cols = slice((j - start) * PAIR, (j - start + 1) * PAIR)
                    out[n, s, :rows, cols] = group_cols(ins[a], s, j, core)
                    out[n, s, rows:, cols] = got[first + a, s, :, j * PAIR : (j + 1) * PAIR]


def join_rows(meta, arrays, got, pieces, first):
    seqs, rows, _ = arrays[0].shape
    count = len(arrays)
    part = pl.BlockSpec((6, seqs, rows, GROUP), lambda: (0, 0, 0, 0))
    return pl.pallas_call(
        functools.partial(join_body, pieces=pieces, first=first),
        out_shape=[
            jax.ShapeDtypeStruct((len(src), seqs, 2 * rows, (stop - start) * PAIR), BF)
            for src, (start, stop) in pieces
        ],
        in_specs=[smem_spec()] + [vmem_spec()] * count + [part],
        out_specs=[vmem_spec()] * len(pieces),
        compiler_params=params(),
        cost_estimate=COSTS["join"],
    )(meta, *arrays, got)


def key_bias(meta):
    core, chunk = meta[0], meta[1]
    span = 2 * 64
    shape = (span, 3 * span)
    rows = lax.broadcasted_iota(jnp.int32, shape, 0)
    cols = lax.broadcasted_iota(jnp.int32, shape, 1)
    q_pos = (rows + 64 * core) & (span - 1)
    k_pos = (cols + 64 * core) & (span - 1)
    block = cols >> 7
    before = (block == 0) & (k_pos >= q_pos) & (chunk > 0)
    behind = (block == 2) & (k_pos <= q_pos) & (chunk < COUNT // NC - 1)
    return jnp.where(before | (block == 1) | behind, 0.0, -1e30)


def probs_of(scores, bias):
    scores = scores + bias
    top = jnp.max(scores, axis=-1, keepdims=True)
    terms = jnp.exp2((scores - top) * (SCALE * LOG2E))
    return terms * (1.0 / jnp.sum(terms, axis=-1, keepdims=True))


def rows_of(refs, a, cols):
    return jnp.concatenate([ref[a, 0, :, cols] for ref in refs], axis=0)


def attend_body(meta, q_ref, left, mid, right, quarter, wide):
    bias = key_bias(meta)
    keyed = (left, mid, right)
    for n in range(GROUP // HD):
        cols = slice(n * HD, (n + 1) * HD)
        probs = probs_of(nt(q_ref[0, 0, :, cols], rows_of(keyed, 0, cols)), bias)
        att = nn(probs.astype(BF), rows_of(keyed, 1, cols)).astype(BF)
        quarter[n // 2, 0, :, (n % 2) * HD : (n % 2 + 1) * HD] = att
        wide[0, :, cols] = att


def attend(meta, q_rows, keyed):
    _, seqs, rows, _ = q_rows.shape
    pair = pl.BlockSpec((2, 1, rows, GROUP), lambda s, m: (0, s, 0, 0))
    return pl.pallas_call(
        attend_body,
        out_shape=[
            jax.ShapeDtypeStruct((NJ, seqs, rows, PAIR), BF),
            jax.ShapeDtypeStruct((seqs, rows, GROUP), BF),
        ],
        grid_spec=pltpu.PrefetchScalarGridSpec(
            num_scalar_prefetch=1,
            grid=(seqs,),
            in_specs=[pl.BlockSpec((1, 1, rows, GROUP), lambda s, m: (0, s, 0, 0))] + [pair] * 3,
            out_specs=[
                pl.BlockSpec((NJ, 1, rows, PAIR), lambda s, m: (0, s, 0, 0)),
                pl.BlockSpec((1, rows, GROUP), lambda s, m: (s, 0, 0)),
            ],
        ),
        compiler_params=params("arbitrary"),
        cost_estimate=COSTS["attend"],
    )(meta, q_rows, *keyed)


def tangent_body(meta, q_ref, left, mid, right, left_tan, mid_tan, right_tan, wide):
    bias = key_bias(meta)
    keyed, keyed_tan = (left, mid, right), (left_tan, mid_tan, right_tan)
    rows = q_ref.shape[2]
    for n in range(wide.shape[2] // HD):
        cols = slice(n * HD, (n + 1) * HD)
        q, qt = q_ref[0, 0, :, cols], q_ref[1, 0, :, cols]
        both = nt(jnp.concatenate([q, qt], axis=0), rows_of(keyed, 0, cols))
        probs = probs_of(both[:rows], bias)
        tan = (both[rows:] + nt(q, rows_of(keyed_tan, 0, cols))) * SCALE
        probs_tan = probs * (tan - jnp.sum(probs * tan, axis=-1, keepdims=True))
        left_side = jnp.concatenate([probs.astype(BF), probs_tan.astype(BF)], axis=0)
        right_side = jnp.concatenate(
            [rows_of(keyed_tan, 1, cols), rows_of(keyed, 1, cols)], axis=1
        )
        both = nn(left_side, right_side)
        wide[0, :, cols] = (both[:rows, :HD] + both[rows:, HD:]).astype(BF)


def attend_tangent(meta, q_rows, keyed, keyed_tan, piece):
    _, seqs, rows, _ = q_rows.shape
    first, stop = PIECES[piece]
    width = (stop - first) * PAIR
    part = pl.BlockSpec((2, 1, rows, width), lambda s, m: (0, s, 0, first * PAIR // width))
    tall = pl.BlockSpec((2, 1, rows, width), lambda s, m: (0, s, 0, 0))
    return pl.pallas_call(
        tangent_body,
        out_shape=jax.ShapeDtypeStruct((seqs, rows, width), BF),
        grid_spec=pltpu.PrefetchScalarGridSpec(
            num_scalar_prefetch=1,
            grid=(seqs,),
            in_specs=[part] * 4 + [tall] * 3,
            out_specs=pl.BlockSpec((1, rows, width), lambda s, m: (s, 0, 0)),
        ),
        compiler_params=params("arbitrary"),
        cost_estimate=COSTS["tangent"],
    )(meta, q_rows, *keyed, *keyed_tan)


def gate_rows(ref, rows):
    return jnp.concatenate(
        [jnp.broadcast_to(ref[s : s + 1, :], (rows, ref.shape[1])) for s in range(2)], axis=0
    )


def flat2(ref):
    return ref[...].reshape(ref.shape[0] * ref.shape[1], ref.shape[2])


def put_halves(value, here, other, at):
    rows = here.shape[-2]
    for s in range(2):
        here[at, s] = value[2 * s * rows : (2 * s + 1) * rows]
        other[at, s] = value[(2 * s + 1) * rows : (2 * s + 2) * rows]


def project_body(att, tan, weight, gate, gate_tan, here, other):
    rows = att.shape[1]
    proj = nt(flat2(att), weight[...])
    proj_tan = nt(flat2(tan), weight[:, : tan.shape[2]])
    g, gt = gate_rows(gate, rows), gate_rows(gate_tan, rows)
    put_halves(g * proj, here, other, 0)
    put_halves(gt * proj + g * proj_tan, here, other, 1)


def project(att, tan, weight, gate, gate_tan):
    seqs, rows, _ = att.shape
    width = gate.shape[1]
    step = 512
    gates = pl.BlockSpec((2, step), lambda i: (0, i))
    block = pl.BlockSpec((2, seqs, rows // 2, step), lambda i: (0, 0, 0, i))
    return pl.pallas_call(
        project_body,
        grid=(width // step,),
        out_shape=[jax.ShapeDtypeStruct((2, seqs, rows // 2, width), F32)] * 2,
        in_specs=[vmem_spec()] * 2
        + [pl.BlockSpec((step, GROUP), lambda i: (i, 0)), gates, gates],
        out_specs=[block, block],
        compiler_params=params("arbitrary"),
        cost_estimate=COSTS["project"],
    )(att, tan, weight, gate, gate_tan)


def finish_body(tan, weight, gate, here, other):
    proj_tan = nt(flat2(tan), weight[...])
    put_halves(gate_rows(gate, tan.shape[1]) * proj_tan, here, other, 0)


def finish(tan, weight, gate):
    seqs, rows, half = tan.shape
    width = gate.shape[1]
    step = 512
    block = pl.BlockSpec((1, seqs, rows // 2, step), lambda i: (0, 0, 0, i))
    return pl.pallas_call(
        finish_body,
        grid=(width // step,),
        out_shape=[jax.ShapeDtypeStruct((1, seqs, rows // 2, width), F32)] * 2,
        in_specs=[
            vmem_spec(),
            pl.BlockSpec((step, half), lambda i: (i, 1)),
            pl.BlockSpec((2, step), lambda i: (0, i)),
        ],
        out_specs=[block, block],
        compiler_params=params("arbitrary"),
        cost_estimate=COSTS["finish"],
    )(tan, weight, gate)


def grad_body(w_own, w_sib, att, out):
    half = att.shape[2] // 2
    total = None
    for x in range(NX):
        for side, weighted in enumerate((w_own, w_sib)):
            rows = slice(side * half, (side + 1) * half)
            block = jnp.concatenate([att[x, s, rows] for s in range(2)], axis=0)
            term = nn(weighted[x], block)
            total = term if total is None else total + term
    total = total.astype(BF)
    piece = out.shape[2]
    for yl in range(NYL):
        for z in range(NZ):
            start = (yl * NZ + z) * piece
            out[z, yl] = total[start : start + piece]


def grad_terms(w_own, w_sib, att):
    width = w_own.shape[1]
    return pl.pallas_call(
        grad_body,
        out_shape=jax.ShapeDtypeStruct((NZ, NYL, width // (NZ * NYL), PAIR), BF),
        in_specs=[vmem_spec()] * 3,
        out_specs=vmem_spec(),
        compiler_params=params(),
        cost_estimate=COSTS["grad"],
    )(w_own, w_sib, att)


def in_order(mine, other, bit):
    return jnp.where(
        bit == 0, jnp.concatenate([mine, other]), jnp.concatenate([other, mine])
    )


def on_device(
    queries, keys, values, query_tan, key_tan, value_tan, weight_out, gate, gate_tan, cotangent
):
    seq_at, uly_at = lax.axis_index("seq"), lax.axis_index("uly")
    core = uly_at % NC
    yl_at = seq_at // (NX * NZ)
    chunk = seq_at * NYH + uly_at // NC
    meta = jnp.stack([core, chunk]).astype(jnp.int32)
    seqs, rows, _ = queries.shape

    arrays = (keys, values, queries, query_tan, key_tan, value_tan)
    got = send(split_groups(meta, arrays), SWAP_CORE, "Sx")
    low = weight_out.astype(BF).reshape(NJ, NC, PAIR, -1)
    low = lax.dynamic_index_in_dim(low, core, 1, keepdims=False).reshape(GROUP, -1).T
    low = in_order(low[None], send(low[None], SWAP_YLO, "Wy"), yl_at)
    got, low = after((got, low))
    (kv,) = join_rows(meta, arrays[:2], got, (((0, 1), (0, NJ)),), 0)
    keyed = (send(kv, TO_NEXT, "Ha"), kv, send(kv, TO_PREV, "Hb"))
    q_rows, *tans = join_rows(
        meta, arrays[2:], got, (((0, 1), (0, NJ)),) + tuple(((2, 3), p) for p in PIECES), 2
    )
    tans = [[send(t, TO_NEXT, "T%da" % n), t, send(t, TO_PREV, "T%db" % n)] for n, t in enumerate(tans)]

    cotangent, _ = after((cotangent, got))
    weighted = (gate[:, None, :] * cotangent.astype(F32)).astype(BF)
    weighted = weighted.reshape(seqs * rows, -1).T
    w_own = lax.all_gather(weighted, AXES, axis_index_groups=GROUPS_X)
    w_own, _ = after((w_own, kv))
    w_sib = send(w_own, SWAP_CORE, "Cswap")

    low = lax.all_gather(low, AXES, axis_index_groups=GROUPS_X, axis=1, tiled=True)
    weight = lax.all_gather(low, AXES, axis_index_groups=GROUPS_Z, axis=1, tiled=True)
    weight = weight.reshape(-1, GROUP)

    quarter, att = attend(meta, q_rows, keyed)
    quarter = lax.all_to_all(quarter, AXES, 0, 0, axis_index_groups=GROUPS_X, tiled=True)
    (quarter, tans[1][0], tans[1][2]) = after((quarter, tans[1][0], tans[1][2]))
    terms = grad_terms(w_own, w_sib, quarter)
    terms = lax.all_to_all(terms, AXES, 0, 0, axis_index_groups=GROUPS_Z, tiled=True)
    terms = jnp.sum(terms.astype(F32), axis=0).reshape(NYL * NYH, -1, PAIR)
    summed = terms
    terms = lax.all_to_all(terms, AXES, 0, 0, axis_index_groups=GROUPS_Y, tiled=True)
    terms = jnp.sum(terms, axis=0)
    weight_grad = send(terms, TURN, "Turn").T

    tan_first = attend_tangent(meta, q_rows, keyed, tans[0], 0)
    att, _ = after((att, summed))
    here, other = project(att, tan_first, weight, gate, gate_tan)
    other = send(other, SWAP_CORE, "Pswap")
    tan_last = attend_tangent(meta, q_rows, keyed, tans[1], 1)
    tan_last, _ = after((tan_last, terms))
    rest, rest_other = finish(tan_last, weight, gate)
    rest_other = send(rest_other, SWAP_CORE, "Uswap")
    mixed = (here[0] + other[0]).astype(BF)
    mixed_tan = ((here[1] + other[1]) + (rest[0] + rest_other[0])).astype(BF)
    return mixed, mixed_tan, weight_grad


def solution(mesh):
    rows = P(None, ("seq", "uly"), None)
    return jax.shard_map(
        on_device,
        mesh=mesh,
        in_specs=(rows,) * 6 + (P(None, "seq"), P(), P(), rows),
        out_specs=(rows, rows, P("uly", "seq")),
        check_vma=False,
    )
```

```python
import functools

import jax
import jax.numpy as jnp
from jax import lax
from jax.experimental import pallas as pl
from jax.experimental.pallas import tpu as pltpu
from jax.sharding import PartitionSpec as P

AXES = ("seq", "uly")
NX, NZ, NYL, NYH, NC = 4, 8, 2, 4, 2
HD = 128
PAIR = 2 * HD
NJ = 4
GROUP = NJ * PAIR
PIECES = ((0, 2), (2, 4))
SCALE = HD ** (-0.5)
LOG2E = 1.4426950408889634
BF = jnp.bfloat16
F32 = jnp.float32


def device_of(x, yl, yh, z, c):
    return ((yl * NZ + z) * NX + x) * (NYH * NC) + yh * NC + c


def all_places():
    for x in range(NX):
        for yl in range(NYL):
            for yh in range(NYH):
                for z in range(NZ):
                    for c in range(NC):
                        yield x, yl, yh, z, c


def moves(rule):
    return sorted((device_of(*p), device_of(*rule(*p))) for p in all_places())


SWAP_CORE = moves(lambda x, yl, yh, z, c: (x, yl, yh, z, 1 - c))
SWAP_YLO = moves(lambda x, yl, yh, z, c: (x, 1 - yl, yh, z, c))
TURN = moves(lambda x, yl, yh, z, c: (yh, yl, x, z, c))


def swap_z(bit):
    return moves(lambda x, yl, yh, z, c: (x, yl, yh, z ^ bit, c))


def shift_x(by):
    return moves(lambda x, yl, yh, z, c: ((x + by) % NX, yl, yh, z, c))


COUNT = NX * NYL * NYH * NZ * NC
TO_NEXT = [(d, d + NC) for d in range(COUNT - NC)]
TO_PREV = [(d + NC, d) for d in range(COUNT - NC)]
GROUPS_X = [
    [device_of(x, yl, yh, z, c) for x in range(NX)]
    for yl in range(NYL) for yh in range(NYH) for z in range(NZ) for c in range(NC)
]
GROUPS_Z = [
    [device_of(x, yl, yh, z, c) for z in range(NZ)]
    for yl in range(NYL) for yh in range(NYH) for x in range(NX) for c in range(NC)
]
GROUPS_Y = [
    [device_of(x, yl, yh, z, c) for yl in range(NYL) for yh in range(NYH)]
    for z in range(NZ) for x in range(NX) for c in range(NC)
]


def send(array, pairs, tag):
    with jax.named_scope(tag):
        return lax.ppermute(array, AXES, pairs)


def after(values):
    return lax.optimization_barrier(values)


def nt(left, right):
    return lax.dot_general(left, right, (((1,), (1,)), ((), ())), preferred_element_type=F32)


def nn(left, right):
    return lax.dot_general(left, right, (((1,), (0,)), ((), ())), preferred_element_type=F32)


def vmem_spec():
    return pl.BlockSpec(memory_space=pltpu.VMEM)


def smem_spec():
    return pl.BlockSpec(memory_space=pltpu.SMEM)


def params(*semantics):
    return pltpu.CompilerParams(
        vmem_limit_bytes=60 * 2**20, dimension_semantics=semantics or None
    )


def cost(flops, nbytes, trans=0):
    return pl.CostEstimate(flops=flops, bytes_accessed=nbytes, transcendentals=trans)


COSTS = dict(
    split=cost(1, 1),
    join=cost(1, 1),
    attend=cost(2**37, 1),
    tangent=cost(1, 1),
    project=cost(1, 1),
    grad=cost(1, 1),
)


def group_cols(ref, s, j, side):
    return ref[s, :, pl.ds(pl.multiple_of(j * 2 * PAIR + side * PAIR, PAIR), PAIR)]


def split_body(meta, *refs):
    core = meta[0]
    ins, out = refs[:-1], refs[-1]
    for a, ref in enumerate(ins):
        for s in range(2):
            for j in range(NJ):
                out[a, s, :, j * PAIR : (j + 1) * PAIR] = group_cols(ref, s, j, 1 - core)


def split_groups(meta, arrays):
    count = len(arrays)
    seqs, rows, _ = arrays[0].shape
    return pl.pallas_call(
        split_body,
        out_shape=jax.ShapeDtypeStruct((count, seqs, rows, GROUP), BF),
        in_specs=[smem_spec()] + [vmem_spec()] * count,
        out_specs=vmem_spec(),
        compiler_params=params(),
        cost_estimate=COSTS["split"],
    )(meta, *arrays)


def join_body(meta, *refs, pieces, first):
    core = meta[0]
    count = len(refs) - 1 - len(pieces)
    ins, got, outs = refs[:count], refs[count], refs[count + 1 :]
    rows = ins[0].shape[1]
    for out, (sources, (start, stop)) in zip(outs, pieces):
        for n, a in enumerate(sources):
            for s in range(2):
                for j in range(start, stop):
                    cols = slice((j - start) * PAIR, (j - start + 1) * PAIR)
                    out[n, s, :rows, cols] = group_cols(ins[a], s, j, core)
                    out[n, s, rows:, cols] = got[first + a, s, :, j * PAIR : (j + 1) * PAIR]


def join_rows(meta, arrays, got, pieces, first):
    seqs, rows, _ = arrays[0].shape
    count = len(arrays)
    part = pl.BlockSpec((6, seqs, rows, GROUP), lambda: (0, 0, 0, 0))
    return pl.pallas_call(
        functools.partial(join_body, pieces=pieces, first=first),
        out_shape=[
            jax.ShapeDtypeStruct((len(src), seqs, 2 * rows, (stop - start) * PAIR), BF)
            for src, (start, stop) in pieces
        ],
        in_specs=[smem_spec()] + [vmem_spec()] * count + [part],
        out_specs=[vmem_spec()] * len(pieces),
        compiler_params=params(),
        cost_estimate=COSTS["join"],
    )(meta, *arrays, got)


def key_bias(meta):
    core, chunk = meta[0], meta[1]
    span = 2 * 64
    shape = (span, 3 * span)
    rows = lax.broadcasted_iota(jnp.int32, shape, 0)
    cols = lax.broadcasted_iota(jnp.int32, shape, 1)
    q_pos = (rows + 64 * core) & (span - 1)
    k_pos = (cols + 64 * core) & (span - 1)
    block = cols >> 7
    before = (block == 0) & (k_pos >= q_pos) & (chunk > 0)
    behind = (block == 2) & (k_pos <= q_pos) & (chunk < COUNT // NC - 1)
    return jnp.where(before | (block == 1) | behind, 0.0, -1e30)


def probs_of(scores, bias):
    scores = scores + bias
    top = jnp.max(scores, axis=-1, keepdims=True)
    terms = jnp.exp2((scores - top) * (SCALE * LOG2E))
    return terms * (1.0 / jnp.sum(terms, axis=-1, keepdims=True))


def rows_of(refs, a, cols):
    return jnp.concatenate([ref[a, 0, :, cols] for ref in refs], axis=0)


def attend_body(meta, q_ref, left, mid, right, quarter, wide):
    bias = key_bias(meta)
    keyed = (left, mid, right)
    for n in range(GROUP // HD):
        cols = slice(n * HD, (n + 1) * HD)
        probs = probs_of(nt(q_ref[0, 0, :, cols], rows_of(keyed, 0, cols)), bias)
        att = nn(probs.astype(BF), rows_of(keyed, 1, cols)).astype(BF)
        quarter[n // 2, 0, :, (n % 2) * HD : (n % 2 + 1) * HD] = att
        wide[0, :, cols] = att


def attend(meta, q_rows, keyed):
    _, seqs, rows, _ = q_rows.shape
    pair = pl.BlockSpec((2, 1, rows, GROUP), lambda s, m: (0, s, 0, 0))
    return pl.pallas_call(
        attend_body,
        out_shape=[
            jax.ShapeDtypeStruct((NJ, seqs, rows, PAIR), BF),
            jax.ShapeDtypeStruct((seqs, rows, GROUP), BF),
        ],
        grid_spec=pltpu.PrefetchScalarGridSpec(
            num_scalar_prefetch=1,
            grid=(seqs,),
            in_specs=[pl.BlockSpec((1, 1, rows, GROUP), lambda s, m: (0, s, 0, 0))] + [pair] * 3,
            out_specs=[
                pl.BlockSpec((NJ, 1, rows, PAIR), lambda s, m: (0, s, 0, 0)),
                pl.BlockSpec((1, rows, GROUP), lambda s, m: (s, 0, 0)),
            ],
        ),
        compiler_params=params("arbitrary"),
        cost_estimate=COSTS["attend"],
    )(meta, q_rows, *keyed)


def tangent_body(meta, q_ref, left, mid, right, left_tan, mid_tan, right_tan, wide):
    bias = key_bias(meta)
    keyed, keyed_tan = (left, mid, right), (left_tan, mid_tan, right_tan)
    rows = q_ref.shape[2]
    for n in range(wide.shape[2] // HD):
        cols = slice(n * HD, (n + 1) * HD)
        q, qt = q_ref[0, 0, :, cols], q_ref[1, 0, :, cols]
        both = nt(jnp.concatenate([q, qt], axis=0), rows_of(keyed, 0, cols))
        probs = probs_of(both[:rows], bias)
        tan = (both[rows:] + nt(q, rows_of(keyed_tan, 0, cols))) * SCALE
        probs_tan = probs * (tan - jnp.sum(probs * tan, axis=-1, keepdims=True))
        left_side = jnp.concatenate([probs.astype(BF), probs_tan.astype(BF)], axis=0)
        right_side = jnp.concatenate(
            [rows_of(keyed_tan, 1, cols), rows_of(keyed, 1, cols)], axis=1
        )
        both = nn(left_side, right_side)
        wide[0, :, cols] = (both[:rows, :HD] + both[rows:, HD:]).astype(BF)


def attend_tangent(meta, q_rows, keyed, keyed_tan, piece):
    _, seqs, rows, _ = q_rows.shape
    first, stop = PIECES[piece]
    width = (stop - first) * PAIR
    part = pl.BlockSpec((2, 1, rows, width), lambda s, m: (0, s, 0, first * PAIR // width))
    tall = pl.BlockSpec((2, 1, rows, width), lambda s, m: (0, s, 0, 0))
    return pl.pallas_call(
        tangent_body,
        out_shape=jax.ShapeDtypeStruct((seqs, rows, width), BF),
        grid_spec=pltpu.PrefetchScalarGridSpec(
            num_scalar_prefetch=1,
            grid=(seqs,),
            in_specs=[part] * 4 + [tall] * 3,
            out_specs=pl.BlockSpec((1, rows, width), lambda s, m: (s, 0, 0)),
        ),
        compiler_params=params("arbitrary"),
        cost_estimate=COSTS["tangent"],
    )(meta, q_rows, *keyed, *keyed_tan)


def gate_rows(ref, rows):
    return jnp.concatenate(
        [jnp.broadcast_to(ref[s : s + 1, :], (rows, ref.shape[1])) for s in range(2)], axis=0
    )


def flat2(ref):
    return ref[...].reshape(ref.shape[0] * ref.shape[1], ref.shape[2])


def put_halves(value, here, other, at):
    rows = here.shape[-2]
    for s in range(2):
        here[at, s] = value[2 * s * rows : (2 * s + 1) * rows]
        other[at, s] = value[(2 * s + 1) * rows : (2 * s + 2) * rows]


def project_body(att, first, last, weight, gate, gate_tan, here, other):
    rows = att.shape[1]
    half = first.shape[2]
    proj = nt(flat2(att), weight[...])
    proj_tan = nt(flat2(first), weight[:, :half]) + nt(flat2(last), weight[:, half:])
    g, gt = gate_rows(gate, rows), gate_rows(gate_tan, rows)
    put_halves(g * proj, here, other, 0)
    put_halves(gt * proj + g * proj_tan, here, other, 1)


def project(att, first, last, weight, gate, gate_tan):
    seqs, rows, _ = att.shape
    width = gate.shape[1]
    step = 512
    gates = pl.BlockSpec((2, step), lambda i: (0, i))
    block = pl.BlockSpec((2, seqs, rows // 2, step), lambda i: (0, 0, 0, i))
    return pl.pallas_call(
        project_body,
        grid=(width // step,),
        out_shape=[jax.ShapeDtypeStruct((2, seqs, rows // 2, width), F32)] * 2,
        in_specs=[vmem_spec()] * 3
        + [pl.BlockSpec((step, GROUP), lambda i: (i, 0)), gates, gates],
        out_specs=[block, block],
        compiler_params=params("arbitrary"),
        cost_estimate=COSTS["project"],
    )(att, first, last, weight, gate, gate_tan)


def grad_body(w_own, w_sib, att, out):
    half = att.shape[2] // 2
    total = None
    for x in range(NX):
        for side, weighted in enumerate((w_own, w_sib)):
            rows = slice(side * half, (side + 1) * half)
            block = jnp.concatenate([att[x, s, rows] for s in range(2)], axis=0)
            term = nn(weighted[x], block)
            total = term if total is None else total + term
    total = total.astype(BF)
    piece = out.shape[2]
    for yl in range(NYL):
        for z in range(NZ):
            start = (yl * NZ + z) * piece
            out[z, yl] = total[start : start + piece]


def grad_terms(w_own, w_sib, att):
    width = w_own.shape[1]
    return pl.pallas_call(
        grad_body,
        out_shape=jax.ShapeDtypeStruct((NZ, NYL, width // (NZ * NYL), PAIR), BF),
        in_specs=[vmem_spec()] * 3,
        out_specs=vmem_spec(),
        compiler_params=params(),
        cost_estimate=COSTS["grad"],
    )(w_own, w_sib, att)


def in_order(mine, other, bit):
    return jnp.where(
        bit == 0, jnp.concatenate([mine, other]), jnp.concatenate([other, mine])
    )


def on_device(
    queries, keys, values, query_tan, key_tan, value_tan, weight_out, gate, gate_tan, cotangent
):
    seq_at, uly_at = lax.axis_index("seq"), lax.axis_index("uly")
    core = uly_at % NC
    yl_at = seq_at // (NX * NZ)
    chunk = seq_at * NYH + uly_at // NC
    meta = jnp.stack([core, chunk]).astype(jnp.int32)
    seqs, rows, _ = queries.shape

    arrays = (keys, values, queries, query_tan, key_tan, value_tan)
    got = send(split_groups(meta, arrays), SWAP_CORE, "Sx")
    low = weight_out.astype(BF).reshape(NJ, NC, PAIR, -1)
    low = lax.dynamic_index_in_dim(low, core, 1, keepdims=False).reshape(GROUP, -1).T
    low = in_order(low[None], send(low[None], SWAP_YLO, "Wy"), yl_at)
    got, low = after((got, low))
    (kv,) = join_rows(meta, arrays[:2], got, (((0, 1), (0, NJ)),), 0)
    keyed = (send(kv, TO_NEXT, "Ha"), kv, send(kv, TO_PREV, "Hb"))
    q_rows, *tans = join_rows(
        meta, arrays[2:], got, (((0, 1), (0, NJ)),) + tuple(((2, 3), p) for p in PIECES), 2
    )
    low = lax.all_gather(low, AXES, axis_index_groups=GROUPS_X, axis=1, tiled=True)
    *tans, _ = after((*tans, low))
    tans = [[send(t, TO_NEXT, "T%da" % n), t, send(t, TO_PREV, "T%db" % n)] for n, t in enumerate(tans)]

    cotangent, _ = after((cotangent, got))
    weighted = (gate[:, None, :] * cotangent.astype(F32)).astype(BF)
    weighted = weighted.reshape(seqs * rows, -1).T
    w_own = lax.all_gather(weighted, AXES, axis_index_groups=GROUPS_X)
    w_own, _ = after((w_own, kv))
    w_sib = send(w_own, SWAP_CORE, "Cswap")

    weight = lax.all_gather(low, AXES, axis_index_groups=GROUPS_Z, axis=1, tiled=True)
    weight = weight.reshape(-1, GROUP)

    quarter, att = attend(meta, q_rows, keyed)
    quarter = lax.all_to_all(quarter, AXES, 0, 0, axis_index_groups=GROUPS_X, tiled=True)
    (quarter, tans[0][0], tans[0][2]) = after((quarter, tans[0][0], tans[0][2]))
    terms = grad_terms(w_own, w_sib, quarter)
    terms = lax.all_to_all(terms, AXES, 0, 0, axis_index_groups=GROUPS_Z, tiled=True)
    terms = jnp.sum(terms.astype(F32), axis=0).reshape(NYL * NYH, -1, PAIR)
    terms = lax.all_to_all(terms, AXES, 0, 0, axis_index_groups=GROUPS_Y, tiled=True)
    terms = jnp.sum(terms, axis=0)
    weight_grad = send(terms, TURN, "Turn").T

    first = attend_tangent(meta, q_rows, keyed, tans[0], 0)
    last = attend_tangent(meta, q_rows, keyed, tans[1], 1)
    here, other = project(att, first, last, weight, gate, gate_tan)
    other = send(other, SWAP_CORE, "Pswap")
    mixed = (here[0] + other[0]).astype(BF)
    mixed_tan = (here[1] + other[1]).astype(BF)
    return mixed, mixed_tan, weight_grad


def solution(mesh):
    rows = P(None, ("seq", "uly"), None)
    return jax.shard_map(
        on_device,
        mesh=mesh,
        in_specs=(rows,) * 6 + (P(None, "seq"), P(), P(), rows),
        out_specs=(rows, rows, P("uly", "seq")),
        check_vma=False,
    )
```

```python
import functools

import jax
import jax.numpy as jnp
from jax import lax
from jax.experimental import pallas as pl
from jax.experimental.pallas import tpu as pltpu
from jax.sharding import PartitionSpec as P

AXES = ("seq", "uly")
NX, NZ, NYL, NYH, NC = 4, 8, 2, 4, 2
HD = 128
PAIR = 2 * HD
NJ = 4
GROUP = NJ * PAIR
PIECES = ((0, 2), (2, 4))
SCALE = HD ** (-0.5)
LOG2E = 1.4426950408889634
BF = jnp.bfloat16
F32 = jnp.float32


def device_of(x, yl, yh, z, c):
    return ((yl * NZ + z) * NX + x) * (NYH * NC) + yh * NC + c


def all_places():
    for x in range(NX):
        for yl in range(NYL):
            for yh in range(NYH):
                for z in range(NZ):
                    for c in range(NC):
                        yield x, yl, yh, z, c


def moves(rule):
    return sorted((device_of(*p), device_of(*rule(*p))) for p in all_places())


SWAP_CORE = moves(lambda x, yl, yh, z, c: (x, yl, yh, z, 1 - c))
SWAP_YLO = moves(lambda x, yl, yh, z, c: (x, 1 - yl, yh, z, c))
TURN = moves(lambda x, yl, yh, z, c: (yh, yl, x, z, c))


def swap_z(bit):
    return moves(lambda x, yl, yh, z, c: (x, yl, yh, z ^ bit, c))


def shift_x(by):
    return moves(lambda x, yl, yh, z, c: ((x + by) % NX, yl, yh, z, c))


COUNT = NX * NYL * NYH * NZ * NC
TO_NEXT = [(d, d + NC) for d in range(COUNT - NC)]
TO_PREV = [(d + NC, d) for d in range(COUNT - NC)]
GROUPS_X = [
    [device_of(x, yl, yh, z, c) for x in range(NX)]
    for yl in range(NYL) for yh in range(NYH) for z in range(NZ) for c in range(NC)
]
GROUPS_Z = [
    [device_of(x, yl, yh, z, c) for z in range(NZ)]
    for yl in range(NYL) for yh in range(NYH) for x in range(NX) for c in range(NC)
]
GROUPS_Y = [
    [device_of(x, yl, yh, z, c) for yl in range(NYL) for yh in range(NYH)]
    for z in range(NZ) for x in range(NX) for c in range(NC)
]


def send(array, pairs, tag):
    with jax.named_scope(tag):
        return lax.ppermute(array, AXES, pairs)


def after(values):
    return lax.optimization_barrier(values)


def nt(left, right):
    return lax.dot_general(left, right, (((1,), (1,)), ((), ())), preferred_element_type=F32)


def nn(left, right):
    return lax.dot_general(left, right, (((1,), (0,)), ((), ())), preferred_element_type=F32)


def vmem_spec():
    return pl.BlockSpec(memory_space=pltpu.VMEM)


def smem_spec():
    return pl.BlockSpec(memory_space=pltpu.SMEM)


def params(*semantics):
    return pltpu.CompilerParams(
        vmem_limit_bytes=60 * 2**20, dimension_semantics=semantics or None
    )


def cost(flops, nbytes, trans=0):
    return pl.CostEstimate(flops=flops, bytes_accessed=nbytes, transcendentals=trans)


COSTS = dict(
    split=cost(1, 1),
    join=cost(1, 1),
    attend=cost(2**37, 1),
    tangent=cost(1, 1),
    project=cost(1, 1),
    grad=cost(1, 1),
)


def group_cols(ref, s, j, side):
    return ref[s, :, pl.ds(pl.multiple_of(j * 2 * PAIR + side * PAIR, PAIR), PAIR)]


def split_body(meta, *refs):
    core = meta[0]
    ins, out = refs[:-1], refs[-1]
    for a, ref in enumerate(ins):
        for s in range(2):
            for j in range(NJ):
                out[a, s, :, j * PAIR : (j + 1) * PAIR] = group_cols(ref, s, j, 1 - core)


def split_groups(meta, arrays):
    count = len(arrays)
    seqs, rows, _ = arrays[0].shape
    return pl.pallas_call(
        split_body,
        out_shape=jax.ShapeDtypeStruct((count, seqs, rows, GROUP), BF),
        in_specs=[smem_spec()] + [vmem_spec()] * count,
        out_specs=vmem_spec(),
        compiler_params=params(),
        cost_estimate=COSTS["split"],
    )(meta, *arrays)


def join_body(meta, *refs, pieces, first):
    core = meta[0]
    count = len(refs) - 1 - len(pieces)
    ins, got, outs = refs[:count], refs[count], refs[count + 1 :]
    rows = ins[0].shape[1]
    for out, (sources, (start, stop)) in zip(outs, pieces):
        for n, a in enumerate(sources):
            for s in range(2):
                for j in range(start, stop):
                    cols = slice((j - start) * PAIR, (j - start + 1) * PAIR)
                    out[n, s, :rows, cols] = group_cols(ins[a], s, j, core)
                    out[n, s, rows:, cols] = got[first + a, s, :, j * PAIR : (j + 1) * PAIR]


def join_rows(meta, arrays, got, pieces, first):
    seqs, rows, _ = arrays[0].shape
    count = len(arrays)
    part = pl.BlockSpec((6, seqs, rows, GROUP), lambda: (0, 0, 0, 0))
    return pl.pallas_call(
        functools.partial(join_body, pieces=pieces, first=first),
        out_shape=[
            jax.ShapeDtypeStruct((len(src), seqs, 2 * rows, (stop - start) * PAIR), BF)
            for src, (start, stop) in pieces
        ],
        in_specs=[smem_spec()] + [vmem_spec()] * count + [part],
        out_specs=[vmem_spec()] * len(pieces),
        compiler_params=params(),
        cost_estimate=COSTS["join"],
    )(meta, *arrays, got)


def key_bias(meta):
    core, chunk = meta[0], meta[1]
    span = 2 * 64
    shape = (span, 3 * span)
    rows = lax.broadcasted_iota(jnp.int32, shape, 0)
    cols = lax.broadcasted_iota(jnp.int32, shape, 1)
    q_pos = (rows + 64 * core) & (span - 1)
    k_pos = (cols + 64 * core) & (span - 1)
    block = cols >> 7
    before = (block == 0) & (k_pos >= q_pos) & (chunk > 0)
    behind = (block == 2) & (k_pos <= q_pos) & (chunk < COUNT // NC - 1)
    return jnp.where(before | (block == 1) | behind, 0.0, -1e30)


def probs_of(scores, bias):
    scores = scores + bias
    top = jnp.max(scores, axis=-1, keepdims=True)
    terms = jnp.exp2((scores - top) * (SCALE * LOG2E))
    return terms * (1.0 / jnp.sum(terms, axis=-1, keepdims=True))


def rows_of(refs, a, cols):
    return jnp.concatenate([ref[a, 0, :, cols] for ref in refs], axis=0)


def attend_body(meta, q_ref, left, mid, right, quarter, wide):
    bias = key_bias(meta)
    keyed = (left, mid, right)
    for n in range(GROUP // HD):
        cols = slice(n * HD, (n + 1) * HD)
        probs = probs_of(nt(q_ref[0, 0, :, cols], rows_of(keyed, 0, cols)), bias)
        att = nn(probs.astype(BF), rows_of(keyed, 1, cols)).astype(BF)
        quarter[n // 2, 0, :, (n % 2) * HD : (n % 2 + 1) * HD] = att
        wide[0, :, cols] = att


def attend(meta, q_rows, keyed):
    _, seqs, rows, _ = q_rows.shape
    pair = pl.BlockSpec((2, 1, rows, GROUP), lambda s, m: (0, s, 0, 0))
    return pl.pallas_call(
        attend_body,
        out_shape=[
            jax.ShapeDtypeStruct((NJ, seqs, rows, PAIR), BF),
            jax.ShapeDtypeStruct((seqs, rows, GROUP), BF),
        ],
        grid_spec=pltpu.PrefetchScalarGridSpec(
            num_scalar_prefetch=1,
            grid=(seqs,),
            in_specs=[pl.BlockSpec((1, 1, rows, GROUP), lambda s, m: (0, s, 0, 0))] + [pair] * 3,
            out_specs=[
                pl.BlockSpec((NJ, 1, rows, PAIR), lambda s, m: (0, s, 0, 0)),
                pl.BlockSpec((1, rows, GROUP), lambda s, m: (s, 0, 0)),
            ],
        ),
        compiler_params=params("arbitrary"),
        cost_estimate=COSTS["attend"],
    )(meta, q_rows, *keyed)


def tangent_body(meta, q_ref, left, mid, right, left_tan, mid_tan, right_tan, wide):
    bias = key_bias(meta)
    keyed, keyed_tan = (left, mid, right), (left_tan, mid_tan, right_tan)
    rows = q_ref.shape[2]
    for n in range(wide.shape[2] // HD):
        cols = slice(n * HD, (n + 1) * HD)
        q, qt = q_ref[0, 0, :, cols], q_ref[1, 0, :, cols]
        both = nt(jnp.concatenate([q, qt], axis=0), rows_of(keyed, 0, cols))
        probs = probs_of(both[:rows], bias)
        tan = (both[rows:] + nt(q, rows_of(keyed_tan, 0, cols))) * SCALE
        probs_tan = probs * (tan - jnp.sum(probs * tan, axis=-1, keepdims=True))
        left_side = jnp.concatenate([probs.astype(BF), probs_tan.astype(BF)], axis=0)
        right_side = jnp.concatenate(
            [rows_of(keyed_tan, 1, cols), rows_of(keyed, 1, cols)], axis=1
        )
        both = nn(left_side, right_side)
        wide[0, :, cols] = (both[:rows, :HD] + both[rows:, HD:]).astype(BF)


def attend_tangent(meta, q_rows, keyed, keyed_tan, piece):
    _, seqs, rows, _ = q_rows.shape
    first, stop = PIECES[piece]
    width = (stop - first) * PAIR
    part = pl.BlockSpec((2, 1, rows, width), lambda s, m: (0, s, 0, first * PAIR // width))
    tall = pl.BlockSpec((2, 1, rows, width), lambda s, m: (0, s, 0, 0))
    return pl.pallas_call(
        tangent_body,
        out_shape=jax.ShapeDtypeStruct((seqs, rows, width), BF),
        grid_spec=pltpu.PrefetchScalarGridSpec(
            num_scalar_prefetch=1,
            grid=(seqs,),
            in_specs=[part] * 4 + [tall] * 3,
            out_specs=pl.BlockSpec((1, rows, width), lambda s, m: (s, 0, 0)),
        ),
        compiler_params=params("arbitrary"),
        cost_estimate=COSTS["tangent"],
    )(meta, q_rows, *keyed, *keyed_tan)


def gate_rows(ref, rows):
    return jnp.concatenate(
        [jnp.broadcast_to(ref[s : s + 1, :], (rows, ref.shape[1])) for s in range(2)], axis=0
    )


def flat2(ref):
    return ref[...].reshape(ref.shape[0] * ref.shape[1], ref.shape[2])


def put_halves(value, here, other, at):
    rows = here.shape[-2]
    for s in range(2):
        here[at, s] = value[2 * s * rows : (2 * s + 1) * rows]
        other[at, s] = value[(2 * s + 1) * rows : (2 * s + 2) * rows]


def project_body(att, first, last, weight, gate, gate_tan, here, other):
    rows = att.shape[1]
    half = first.shape[2]
    proj = nt(flat2(att), weight[...])
    proj_tan = nt(flat2(first), weight[:, :half]) + nt(flat2(last), weight[:, half:])
    g, gt = gate_rows(gate, rows), gate_rows(gate_tan, rows)
    put_halves(g * proj, here, other, 0)
    put_halves(gt * proj + g * proj_tan, here, other, 1)


def project(att, first, last, weight, gate, gate_tan):
    seqs, rows, _ = att.shape
    width = gate.shape[1]
    step = 512
    gates = pl.BlockSpec((2, step), lambda i: (0, i))
    block = pl.BlockSpec((2, seqs, rows // 2, step), lambda i: (0, 0, 0, i))
    return pl.pallas_call(
        project_body,
        grid=(width // step,),
        out_shape=[jax.ShapeDtypeStruct((2, seqs, rows // 2, width), F32)] * 2,
        in_specs=[vmem_spec()] * 3
        + [pl.BlockSpec((step, GROUP), lambda i: (i, 0)), gates, gates],
        out_specs=[block, block],
        compiler_params=params("arbitrary"),
        cost_estimate=COSTS["project"],
    )(att, first, last, weight, gate, gate_tan)


def grad_body(w_own, w_sib, att, out):
    half = att.shape[2] // 2
    total = None
    for x in range(NX):
        for side, weighted in enumerate((w_own, w_sib)):
            rows = slice(side * half, (side + 1) * half)
            block = jnp.concatenate([att[x, s, rows] for s in range(2)], axis=0)
            term = nn(weighted[x], block)
            total = term if total is None else total + term
    total = total.astype(BF)
    piece = out.shape[2]
    for yl in range(NYL):
        for z in range(NZ):
            start = (yl * NZ + z) * piece
            out[z, yl] = total[start : start + piece]


def grad_terms(w_own, w_sib, att):
    width = w_own.shape[1]
    return pl.pallas_call(
        grad_body,
        out_shape=jax.ShapeDtypeStruct((NZ, NYL, width // (NZ * NYL), PAIR), BF),
        in_specs=[vmem_spec()] * 3,
        out_specs=vmem_spec(),
        compiler_params=params(),
        cost_estimate=COSTS["grad"],
    )(w_own, w_sib, att)


def in_order(mine, other, bit):
    return jnp.where(
        bit == 0, jnp.concatenate([mine, other]), jnp.concatenate([other, mine])
    )


def on_device(
    queries, keys, values, query_tan, key_tan, value_tan, weight_out, gate, gate_tan, cotangent
):
    seq_at, uly_at = lax.axis_index("seq"), lax.axis_index("uly")
    core = uly_at % NC
    yl_at = seq_at // (NX * NZ)
    chunk = seq_at * NYH + uly_at // NC
    meta = jnp.stack([core, chunk]).astype(jnp.int32)
    seqs, rows, _ = queries.shape

    arrays = (keys, values, queries, query_tan, key_tan, value_tan)
    got = send(split_groups(meta, arrays), SWAP_CORE, "Sx")
    low = weight_out.astype(BF).reshape(NJ, NC, PAIR, -1)
    low = lax.dynamic_index_in_dim(low, core, 1, keepdims=False).reshape(GROUP, -1).T
    low = in_order(low[None], send(low[None], SWAP_YLO, "Wy"), yl_at)
    got, low = after((got, low))
    (kv,) = join_rows(meta, arrays[:2], got, (((0, 1), (0, NJ)),), 0)
    keyed = (send(kv, TO_NEXT, "Ha"), kv, send(kv, TO_PREV, "Hb"))
    q_rows, *tans = join_rows(
        meta, arrays[2:], got, (((0, 1), (0, NJ)),) + tuple(((2, 3), p) for p in PIECES), 2
    )
    low = lax.all_gather(low, AXES, axis_index_groups=GROUPS_X, axis=1, tiled=True)
    *tans, _ = after((*tans, low))
    tans = [[send(t, TO_NEXT, "T%da" % n), t, send(t, TO_PREV, "T%db" % n)] for n, t in enumerate(tans)]

    cotangent, _ = after((cotangent, got))
    weighted = (gate[:, None, :] * cotangent.astype(F32)).astype(BF)
    weighted = weighted.reshape(seqs * rows, -1).T
    w_own = lax.all_gather(weighted, AXES, axis_index_groups=GROUPS_X)
    w_own, _ = after((w_own, kv))
    w_sib = send(w_own, SWAP_CORE, "Cswap")

    weight = lax.all_gather(low, AXES, axis_index_groups=GROUPS_Z, axis=1, tiled=True)
    weight = weight.reshape(-1, GROUP)

    quarter, att = attend(meta, q_rows, keyed)
    quarter = lax.all_to_all(quarter, AXES, 0, 0, axis_index_groups=GROUPS_X, tiled=True)
    (quarter, tans[0][0], tans[0][2]) = after((quarter, tans[0][0], tans[0][2]))
    terms = grad_terms(w_own, w_sib, quarter)
    terms = lax.all_to_all(terms, AXES, 0, 0, axis_index_groups=GROUPS_Z, tiled=True)
    first = attend_tangent(meta, q_rows, keyed, tans[0], 0)
    last = attend_tangent(meta, q_rows, keyed, tans[1], 1)
    terms, first = after((terms, first))
    terms = jnp.sum(terms.astype(F32), axis=0).reshape(NYL * NYH, -1, PAIR)
    terms = lax.all_to_all(terms, AXES, 0, 0, axis_index_groups=GROUPS_Y, tiled=True)
    terms = jnp.sum(terms, axis=0)
    weight_grad = send(terms, TURN, "Turn").T

    att, _ = after((att, terms))
    here, other = project(att, first, last, weight, gate, gate_tan)
    other = send(other, SWAP_CORE, "Pswap")
    mixed = (here[0] + other[0]).astype(BF)
    mixed_tan = (here[1] + other[1]).astype(BF)
    return mixed, mixed_tan, weight_grad


def solution(mesh):
    rows = P(None, ("seq", "uly"), None)
    return jax.shard_map(
        on_device,
        mesh=mesh,
        in_specs=(rows,) * 6 + (P(None, "seq"), P(), P(), rows),
        out_specs=(rows, rows, P("uly", "seq")),
        check_vma=False,
    )
```

```python
import functools

import jax
import jax.numpy as jnp
from jax import lax
from jax.experimental import pallas as pl
from jax.experimental.pallas import tpu as pltpu
from jax.sharding import PartitionSpec as P

AXES = ("seq", "uly")
NX, NZ, NYL, NYH, NC = 4, 8, 2, 4, 2
HD = 128
PAIR = 2 * HD
NJ = 4
GROUP = NJ * PAIR
PIECES = ((0, 2), (2, 4))
SCALE = HD ** (-0.5)
LOG2E = 1.4426950408889634
BF = jnp.bfloat16
F32 = jnp.float32


def device_of(x, yl, yh, z, c):
    return ((yl * NZ + z) * NX + x) * (NYH * NC) + yh * NC + c


def all_places():
    for x in range(NX):
        for yl in range(NYL):
            for yh in range(NYH):
                for z in range(NZ):
                    for c in range(NC):
                        yield x, yl, yh, z, c


def moves(rule):
    return sorted((device_of(*p), device_of(*rule(*p))) for p in all_places())


SWAP_CORE = moves(lambda x, yl, yh, z, c: (x, yl, yh, z, 1 - c))
SWAP_YLO = moves(lambda x, yl, yh, z, c: (x, 1 - yl, yh, z, c))
TURN = moves(lambda x, yl, yh, z, c: (yh, yl, x, z, c))


def swap_z(bit):
    return moves(lambda x, yl, yh, z, c: (x, yl, yh, z ^ bit, c))


def shift_x(by):
    return moves(lambda x, yl, yh, z, c: ((x + by) % NX, yl, yh, z, c))


COUNT = NX * NYL * NYH * NZ * NC
TO_NEXT = [(d, d + NC) for d in range(COUNT - NC)]
TO_PREV = [(d + NC, d) for d in range(COUNT - NC)]
GROUPS_X = [
    [device_of(x, yl, yh, z, c) for x in range(NX)]
    for yl in range(NYL) for yh in range(NYH) for z in range(NZ) for c in range(NC)
]
GROUPS_Z = [
    [device_of(x, yl, yh, z, c) for z in range(NZ)]
    for yl in range(NYL) for yh in range(NYH) for x in range(NX) for c in range(NC)
]
GROUPS_ZYL = [
    [device_of(x, yl, yh, z, c) for yl in range(NYL) for z in range(NZ)]
    for yh in range(NYH) for x in range(NX) for c in range(NC)
]
GROUPS_Y = [
    [device_of(x, yl, yh, z, c) for yl in range(NYL) for yh in range(NYH)]
    for z in range(NZ) for x in range(NX) for c in range(NC)
]


def send(array, pairs, tag):
    with jax.named_scope(tag):
        return lax.ppermute(array, AXES, pairs)


def after(values):
    return lax.optimization_barrier(values)


def nt(left, right):
    return lax.dot_general(left, right, (((1,), (1,)), ((), ())), preferred_element_type=F32)


def nn(left, right):
    return lax.dot_general(left, right, (((1,), (0,)), ((), ())), preferred_element_type=F32)


def vmem_spec():
    return pl.BlockSpec(memory_space=pltpu.VMEM)


def smem_spec():
    return pl.BlockSpec(memory_space=pltpu.SMEM)


def params(*semantics):
    return pltpu.CompilerParams(
        vmem_limit_bytes=60 * 2**20, dimension_semantics=semantics or None
    )


def cost(flops, nbytes, trans=0):
    return pl.CostEstimate(flops=flops, bytes_accessed=nbytes, transcendentals=trans)


COSTS = dict(
    split=cost(1, 1),
    join=cost(1, 1),
    attend=cost(2**37, 1),
    tangent=cost(1, 1),
    project=cost(1, 1),
    grad=cost(1, 1),
)


def group_cols(ref, s, j, side):
    return ref[s, :, pl.ds(pl.multiple_of(j * 2 * PAIR + side * PAIR, PAIR), PAIR)]


def split_body(meta, *refs):
    core = meta[0]
    ins, out = refs[:-1], refs[-1]
    for a, ref in enumerate(ins):
        for s in range(2):
            for j in range(NJ):
                out[a, s, :, j * PAIR : (j + 1) * PAIR] = group_cols(ref, s, j, 1 - core)


def split_groups(meta, arrays):
    count = len(arrays)
    seqs, rows, _ = arrays[0].shape
    return pl.pallas_call(
        split_body,
        out_shape=jax.ShapeDtypeStruct((count, seqs, rows, GROUP), BF),
        in_specs=[smem_spec()] + [vmem_spec()] * count,
        out_specs=vmem_spec(),
        compiler_params=params(),
        cost_estimate=COSTS["split"],
    )(meta, *arrays)


def join_body(meta, *refs, pieces, first):
    core = meta[0]
    count = len(refs) - 1 - len(pieces)
    ins, got, outs = refs[:count], refs[count], refs[count + 1 :]
    rows = ins[0].shape[1]
    for out, (sources, (start, stop)) in zip(outs, pieces):
        for n, a in enumerate(sources):
            for s in range(2):
                for j in range(start, stop):
                    cols = slice((j - start) * PAIR, (j - start + 1) * PAIR)
                    out[n, s, :rows, cols] = group_cols(ins[a], s, j, core)
                    out[n, s, rows:, cols] = got[first + a, s, :, j * PAIR : (j + 1) * PAIR]


def join_rows(meta, arrays, got, pieces, first):
    seqs, rows, _ = arrays[0].shape
    count = len(arrays)
    part = pl.BlockSpec((6, seqs, rows, GROUP), lambda: (0, 0, 0, 0))
    return pl.pallas_call(
        functools.partial(join_body, pieces=pieces, first=first),
        out_shape=[
            jax.ShapeDtypeStruct((len(src), seqs, 2 * rows, (stop - start) * PAIR), BF)
            for src, (start, stop) in pieces
        ],
        in_specs=[smem_spec()] + [vmem_spec()] * count + [part],
        out_specs=[vmem_spec()] * len(pieces),
        compiler_params=params(),
        cost_estimate=COSTS["join"],
    )(meta, *arrays, got)


def key_bias(meta):
    core, chunk = meta[0], meta[1]
    span = 2 * 64
    shape = (span, 3 * span)
    rows = lax.broadcasted_iota(jnp.int32, shape, 0)
    cols = lax.broadcasted_iota(jnp.int32, shape, 1)
    q_pos = (rows + 64 * core) & (span - 1)
    k_pos = (cols + 64 * core) & (span - 1)
    block = cols >> 7
    before = (block == 0) & (k_pos >= q_pos) & (chunk > 0)
    behind = (block == 2) & (k_pos <= q_pos) & (chunk < COUNT // NC - 1)
    return jnp.where(before | (block == 1) | behind, 0.0, -1e30)


def probs_of(scores, bias):
    scores = scores + bias
    top = jnp.max(scores, axis=-1, keepdims=True)
    terms = jnp.exp2((scores - top) * (SCALE * LOG2E))
    return terms * (1.0 / jnp.sum(terms, axis=-1, keepdims=True))


def rows_of(refs, a, cols):
    return jnp.concatenate([ref[a, 0, :, cols] for ref in refs], axis=0)


def attend_body(meta, q_ref, left, mid, right, quarter, wide):
    bias = key_bias(meta)
    keyed = (left, mid, right)
    for n in range(GROUP // HD):
        cols = slice(n * HD, (n + 1) * HD)
        probs = probs_of(nt(q_ref[0, 0, :, cols], rows_of(keyed, 0, cols)), bias)
        att = nn(probs.astype(BF), rows_of(keyed, 1, cols)).astype(BF)
        quarter[n // 2, 0, :, (n % 2) * HD : (n % 2 + 1) * HD] = att
        wide[0, :, cols] = att


def attend(meta, q_rows, keyed):
    _, seqs, rows, _ = q_rows.shape
    pair = pl.BlockSpec((2, 1, rows, GROUP), lambda s, m: (0, s, 0, 0))
    return pl.pallas_call(
        attend_body,
        out_shape=[
            jax.ShapeDtypeStruct((NJ, seqs, rows, PAIR), BF),
            jax.ShapeDtypeStruct((seqs, rows, GROUP), BF),
        ],
        grid_spec=pltpu.PrefetchScalarGridSpec(
            num_scalar_prefetch=1,
            grid=(seqs,),
            in_specs=[pl.BlockSpec((1, 1, rows, GROUP), lambda s, m: (0, s, 0, 0))] + [pair] * 3,
            out_specs=[
                pl.BlockSpec((NJ, 1, rows, PAIR), lambda s, m: (0, s, 0, 0)),
                pl.BlockSpec((1, rows, GROUP), lambda s, m: (s, 0, 0)),
            ],
        ),
        compiler_params=params("arbitrary"),
        cost_estimate=COSTS["attend"],
    )(meta, q_rows, *keyed)


def tangent_body(meta, q_ref, left, mid, right, left_tan, mid_tan, right_tan, wide):
    bias = key_bias(meta)
    keyed, keyed_tan = (left, mid, right), (left_tan, mid_tan, right_tan)
    rows = q_ref.shape[2]
    for n in range(wide.shape[2] // HD):
        cols = slice(n * HD, (n + 1) * HD)
        q, qt = q_ref[0, 0, :, cols], q_ref[1, 0, :, cols]
        both = nt(jnp.concatenate([q, qt], axis=0), rows_of(keyed, 0, cols))
        probs = probs_of(both[:rows], bias)
        tan = (both[rows:] + nt(q, rows_of(keyed_tan, 0, cols))) * SCALE
        probs_tan = probs * (tan - jnp.sum(probs * tan, axis=-1, keepdims=True))
        left_side = jnp.concatenate([probs.astype(BF), probs_tan.astype(BF)], axis=0)
        right_side = jnp.concatenate(
            [rows_of(keyed_tan, 1, cols), rows_of(keyed, 1, cols)], axis=1
        )
        both = nn(left_side, right_side)
        wide[0, :, cols] = (both[:rows, :HD] + both[rows:, HD:]).astype(BF)


def attend_tangent(meta, q_rows, keyed, keyed_tan, piece):
    _, seqs, rows, _ = q_rows.shape
    first, stop = PIECES[piece]
    width = (stop - first) * PAIR
    part = pl.BlockSpec((2, 1, rows, width), lambda s, m: (0, s, 0, first * PAIR // width))
    tall = pl.BlockSpec((2, 1, rows, width), lambda s, m: (0, s, 0, 0))
    return pl.pallas_call(
        tangent_body,
        out_shape=jax.ShapeDtypeStruct((seqs, rows, width), BF),
        grid_spec=pltpu.PrefetchScalarGridSpec(
            num_scalar_prefetch=1,
            grid=(seqs,),
            in_specs=[part] * 4 + [tall] * 3,
            out_specs=pl.BlockSpec((1, rows, width), lambda s, m: (s, 0, 0)),
        ),
        compiler_params=params("arbitrary"),
        cost_estimate=COSTS["tangent"],
    )(meta, q_rows, *keyed, *keyed_tan)


def gate_rows(ref, rows):
    return jnp.concatenate(
        [jnp.broadcast_to(ref[s : s + 1, :], (rows, ref.shape[1])) for s in range(2)], axis=0
    )


def flat2(ref):
    return ref[...].reshape(ref.shape[0] * ref.shape[1], ref.shape[2])


def put_halves(value, here, other, at):
    rows = here.shape[-2]
    for s in range(2):
        here[at, s] = value[2 * s * rows : (2 * s + 1) * rows]
        other[at, s] = value[(2 * s + 1) * rows : (2 * s + 2) * rows]


def project_body(att, first, last, weight, gate, gate_tan, here, other):
    rows = att.shape[1]
    half = first.shape[2]
    proj = nt(flat2(att), weight[...])
    proj_tan = nt(flat2(first), weight[:, :half]) + nt(flat2(last), weight[:, half:])
    g, gt = gate_rows(gate, rows), gate_rows(gate_tan, rows)
    put_halves(g * proj, here, other, 0)
    put_halves(gt * proj + g * proj_tan, here, other, 1)


def project(att, first, last, weight, gate, gate_tan):
    seqs, rows, _ = att.shape
    width = gate.shape[1]
    step = 512
    gates = pl.BlockSpec((2, step), lambda i: (0, i))
    block = pl.BlockSpec((2, seqs, rows // 2, step), lambda i: (0, 0, 0, i))
    return pl.pallas_call(
        project_body,
        grid=(width // step,),
        out_shape=[jax.ShapeDtypeStruct((2, seqs, rows // 2, width), F32)] * 2,
        in_specs=[vmem_spec()] * 3
        + [pl.BlockSpec((step, GROUP), lambda i: (i, 0)), gates, gates],
        out_specs=[block, block],
        compiler_params=params("arbitrary"),
        cost_estimate=COSTS["project"],
    )(att, first, last, weight, gate, gate_tan)


def grad_body(w_own, w_sib, att, out):
    half = att.shape[2] // 2
    total = None
    for x in range(NX):
        for side, weighted in enumerate((w_own, w_sib)):
            rows = slice(side * half, (side + 1) * half)
            block = jnp.concatenate([att[x, s, rows] for s in range(2)], axis=0)
            term = nn(weighted[x], block)
            total = term if total is None else total + term
    total = total.astype(BF)
    piece = out.shape[2]
    for yl in range(NYL):
        for z in range(NZ):
            start = (yl * NZ + z) * piece
            out[z, yl] = total[start : start + piece]


def grad_terms(w_own, w_sib, att):
    width = w_own.shape[1]
    return pl.pallas_call(
        grad_body,
        out_shape=jax.ShapeDtypeStruct((NZ, NYL, width // (NZ * NYL), PAIR), BF),
        in_specs=[vmem_spec()] * 3,
        out_specs=vmem_spec(),
        compiler_params=params(),
        cost_estimate=COSTS["grad"],
    )(w_own, w_sib, att)


def in_order(mine, other, bit):
    return jnp.where(
        bit == 0, jnp.concatenate([mine, other]), jnp.concatenate([other, mine])
    )


def on_device(
    queries, keys, values, query_tan, key_tan, value_tan, weight_out, gate, gate_tan, cotangent
):
    seq_at, uly_at = lax.axis_index("seq"), lax.axis_index("uly")
    core = uly_at % NC
    yl_at = seq_at // (NX * NZ)
    chunk = seq_at * NYH + uly_at // NC
    meta = jnp.stack([core, chunk]).astype(jnp.int32)
    seqs, rows, _ = queries.shape

    arrays = (keys, values, queries, query_tan, key_tan, value_tan)
    got = send(split_groups(meta, arrays), SWAP_CORE, "Sx")
    low = weight_out.astype(BF).reshape(NJ, NC, PAIR, -1)
    low = lax.dynamic_index_in_dim(low, core, 1, keepdims=False).reshape(GROUP, -1).T
    low = jnp.broadcast_to(low[None], (NYL * NZ,) + low.shape)
    low = lax.all_to_all(low, AXES, 0, 0, axis_index_groups=GROUPS_ZYL, tiled=True)
    (kv,) = join_rows(meta, arrays[:2], got, (((0, 1), (0, NJ)),), 0)
    keyed = (send(kv, TO_NEXT, "Ha"), kv, send(kv, TO_PREV, "Hb"))
    q_rows, *tans = join_rows(
        meta, arrays[2:], got, (((0, 1), (0, NJ)),) + tuple(((2, 3), p) for p in PIECES), 2
    )
    *tans, _ = after((*tans, low))
    tans = [[send(t, TO_NEXT, "T%da" % n), t, send(t, TO_PREV, "T%db" % n)] for n, t in enumerate(tans)]

    cotangent, _ = after((cotangent, got))
    weighted = (gate[:, None, :] * cotangent.astype(F32)).astype(BF)
    weighted = weighted.reshape(seqs * rows, -1).T
    w_own = lax.all_gather(weighted, AXES, axis_index_groups=GROUPS_X)
    w_own, _ = after((w_own, kv))
    w_sib = send(w_own, SWAP_CORE, "Cswap")

    weight = lax.all_gather(low, AXES, axis_index_groups=GROUPS_X, axis=1, tiled=True)
    weight = weight.reshape(-1, GROUP)

    quarter, att = attend(meta, q_rows, keyed)
    quarter = lax.all_to_all(quarter, AXES, 0, 0, axis_index_groups=GROUPS_X, tiled=True)
    (quarter, tans[0][0], tans[0][2]) = after((quarter, tans[0][0], tans[0][2]))
    terms = grad_terms(w_own, w_sib, quarter)
    terms = lax.all_to_all(terms, AXES, 0, 0, axis_index_groups=GROUPS_Z, tiled=True)
    terms = jnp.sum(terms.astype(F32), axis=0).reshape(NYL * NYH, -1, PAIR)
    terms = lax.all_to_all(terms, AXES, 0, 0, axis_index_groups=GROUPS_Y, tiled=True)
    terms = jnp.sum(terms, axis=0)
    weight_grad = send(terms, TURN, "Turn").T

    first = attend_tangent(meta, q_rows, keyed, tans[0], 0)
    last = attend_tangent(meta, q_rows, keyed, tans[1], 1)
    here, other = project(att, first, last, weight, gate, gate_tan)
    other = send(other, SWAP_CORE, "Pswap")
    mixed = (here[0] + other[0]).astype(BF)
    mixed_tan = (here[1] + other[1]).astype(BF)
    return mixed, mixed_tan, weight_grad


def solution(mesh):
    rows = P(None, ("seq", "uly"), None)
    return jax.shard_map(
        on_device,
        mesh=mesh,
        in_specs=(rows,) * 6 + (P(None, "seq"), P(), P(), rows),
        out_specs=(rows, rows, P("uly", "seq")),
        check_vma=False,
    )
```
